1024 devices in a mesh: dp: 4 (over x), expert: 8 (over y_hi, core), tensor: 32 (over z, y_lo).
Axes of the slice: x: 4, y: 8 (y_hi: 4, y_lo: 2; y = y_hi * 2 + y_lo), z: 16, core: 2. Of those that a mesh axis runs over, the one named last changes fastest.
Arguments:
- tokens: bfloat16 [1024, 3072], P(('dp', 'expert'), 'tensor'), may hold values from -6 to 6
- expert_ids: int32 [1024, 2], P(('dp', 'expert')), may hold values from 0 to 7, all different within a row; in each aligned block of 32 rows (0 to 31, 32 to 63, ...) at most 16 rows name the same one
- gate_logits: float32 [1024, 2], P(('dp', 'expert')), may hold values from -6 to 6
- gate_weight: bfloat16 [8, 3072, 8192], P('expert', None, 'tensor'), may hold values from -0.109375 to 0.109375
- up_weight: bfloat16 [8, 3072, 8192], P('expert', None, 'tensor'), may hold values from -0.109375 to 0.109375
- down_weight: bfloat16 [8, 3072, 8192], P('expert', None, 'tensor'), may hold values from -0.0625 to 0.0625
- out_grad: bfloat16 [1024, 3072], P(('dp', 'expert'), 'tensor'), may hold values from -0.59765625 to 0.59765625
Outputs:
- mixed: bfloat16 [1024, 3072], P(('dp', 'expert'), 'tensor')
- input_grad: bfloat16 [1024, 3072], P(('dp', 'expert'), 'tensor')
- logit_grad: float32 [1024, 2], P(('dp', 'expert'))
- gate_grad: bfloat16 [8, 3072, 8192], P('expert', 'dp', 'tensor')
- up_grad: bfloat16 [8, 3072, 8192], P('expert', 'dp', 'tensor')
- down_grad: bfloat16 [8, 3072, 8192], P('expert', 'dp', 'tensor')
The draws below stay inside these ranges and needn't reach their ends.
Inputs may be any that keep to these rules, and one draw needn't show every extreme that they name: `expert_ids`: the two experts of a token differ. Among the 32 tokens of one index of dp and expert (one device's rows), no expert is named more than 16 times, a bound that some block reaches.
All inputs are finite; a program needn't handle non-finite values.
Results may differ from the reference program's by a relative error of at most 0.035.
Values may be sent and summed in bfloat16 or wider, within the bound.
A program may use at most 64 MiB of HBM per device.

```python
import math
import jax
import jax.numpy as jnp
import numpy as np
from jax import lax

D = 3072
FF = 8192
TOK_DEV = 32
SLOT = 16
EXPERTS = 8
TOKENS = 1024
N_DP = 4
N_EXPERT = 8
N_TENSOR = 32


def levels(own_key, dims, cuts, low, largest):
    def one(dim, blocks):
        draws = jax.random.uniform(jax.random.fold_in(jax.random.fold_in(own_key, 6), dim), (blocks,), jnp.float32, low / len(cuts), largest / len(cuts))
        return jnp.repeat(jnp.exp(draws), dims[dim] // blocks).reshape((-1,) + (1,) * (len(dims) - dim - 1))

    level = one(*cuts[0])
    for cut in cuts[1:]:
        level = level * one(*cut)
    return level


def shared_out(own_key, own, number, rows, count, top, limit, lean):
    order = jax.random.permutation(own_key, count)
    heavy_load, common = portions_of(count, rows * top, limit, lean, True), portions_of(count, rows * top, limit, lean, False)
    places = jnp.arange(count)

    def named(lengths, offset_by):
        used = int((lengths > 0).sum())
        fixed = max(1, used // 4)
        moved = fixed + (places - fixed + offset_by * (used - fixed)) % max(1, count - fixed)
        return jnp.zeros((count,), jnp.int32).at[order[jnp.where(places < fixed, places, moved)]].set(jnp.asarray(lengths, jnp.int32))

    lengths = jnp.where(number % 4 == 0, named(heavy_load, number // 4), named(common, number - number // 4 - 1))
    mixed = jax.random.permutation(jax.random.fold_in(own, 3), count)
    giver, sink = mixed[0:count // 2 * 2:2], mixed[1:count // 2 * 2:2]
    slack = jnp.minimum(lengths[giver] - 1, limit - lengths[sink]) // 2
    slack = jnp.where((giver == order[0]) | (sink == order[0]) | (lengths[sink] == 0), 0, jnp.maximum(slack, 0))
    moved = jax.random.randint(jax.random.fold_in(own, 4), (count // 2,), 0, 1 << 20) % (slack + 1)
    lengths = lengths.at[giver].add(-moved).at[sink].add(moved)
    items = jnp.searchsorted(jnp.cumsum(lengths), jnp.arange(rows * top), side="right").astype(jnp.int32)
    listing = items.reshape(top, rows).T
    listing = listing[jax.random.permutation(jax.random.fold_in(own, 1), rows)]
    offset_by = jax.random.randint(jax.random.fold_in(own, 2), (rows, 1), 0, top)
    return jnp.take_along_axis(listing, (jnp.arange(top)[None, :] + offset_by) % top, axis=1)


def portions_of(count, total, limit, skew, full):
    portions = [(1 << 20) // math.isqrt(rank ** skew) + 1 for rank in range(1, count + 1)]
    largest = limit if full else min(limit, max(-(-total // count), total * portions[0] // sum(portions)))
    least = 1 if total - largest >= count - 1 else 0
    given, rest = [largest] + [least] * (count - 1), total - largest - least * (count - 1)
    while rest > 0:
        movable = [i for i in range(1, count) if given[i] < largest] or [i for i in range(1, count) if given[i] < limit]
        pool, budget = sum([portions[i] for i in movable]), rest
        for i in movable:
            addition = min(limit - given[i], max(1, budget * portions[i] // pool), rest)
            given[i] = given[i] + addition
            rest = rest - addition
    return np.array(given)


def bell_draw(stream_key, dims, spread, limit, shards=(), kind=jnp.bfloat16):
    result = jax.random.normal(stream_key, dims, jnp.float32) * spread
    if len(shards) > 0:
        result = levels(stream_key, dims, shards, -0.22, 0.18) * result
    return jnp.clip(result, min=-limit, max=limit).astype(kind)


def setup_inputs(seed: int = 0) -> dict:
    key_of = jax.random.split(jax.random.key(seed), 8)
    tokens = bell_draw(key_of[0], (TOKENS, D), 1.0, 6.0, ((0, 32), (1, 32)))
    expert_ids_keys = jax.random.split(jax.random.fold_in(key_of[1], 1), TOKENS // TOK_DEV)
    expert_ids_turns = jax.random.permutation(jax.random.fold_in(key_of[1], 3), TOKENS // TOK_DEV)
    expert_ids = jax.vmap(lambda own, number: shared_out(jax.random.fold_in(key_of[1], 2), own, number, TOK_DEV, EXPERTS, 2, SLOT, 2))(expert_ids_keys, expert_ids_turns).reshape((TOKENS, 2))
    gate_logits = bell_draw(key_of[2], (TOKENS, 2), 1.5, 6.0, ((0, 32),), jnp.float32)
    gate_weight = bell_draw(key_of[3], (EXPERTS, D, FF), D ** -0.5, 0.109375, ((0, 8), (2, 32)))
    up_weight = bell_draw(key_of[4], (EXPERTS, D, FF), D ** -0.5, 0.109375, ((0, 8), (2, 32)))
    down_weight = bell_draw(key_of[5], (EXPERTS, D, FF), FF ** -0.5, 0.0625, ((0, 8), (2, 32)))
    out_grad = bell_draw(key_of[6], (TOKENS, D), 0.1, 0.59765625, ((0, 32), (1, 32)))
    return dict(tokens=tokens, expert_ids=expert_ids, gate_logits=gate_logits, gate_weight=gate_weight, up_weight=up_weight, down_weight=down_weight, out_grad=out_grad)


def slot_targets(expert_ids, expert_total, slot_count, group_rows):
    flat_ids = expert_ids.reshape(-1, group_rows * 2)
    one_hot = (flat_ids[:, :, None] == jnp.arange(expert_total, dtype=jnp.int32)[None, None, :]).astype(jnp.int32)
    earlier = jnp.cumsum(one_hot, axis=1) - one_hot
    position = jnp.sum(earlier * one_hot, axis=2)
    return (flat_ids * slot_count + position).astype(jnp.int32)


def block_sum(left, right):
    parts = jnp.einsum("rjf,djf->rjd", left.astype(jnp.float32), right.astype(jnp.float32), precision=lax.Precision.HIGHEST)
    return parts


def expert_pass(items):
    rows_x, rows_g, w_gate, w_up, w_down = items
    block_width = FF // N_TENSOR
    flat_x = rows_x.reshape(-1, D)
    flat_g = rows_g.reshape(-1, D)
    gate_val = jnp.dot(flat_x, w_gate, preferred_element_type=jnp.float32)
    up_val = jnp.dot(flat_x, w_up, preferred_element_type=jnp.float32)
    sigma = jax.nn.sigmoid(gate_val)
    active = gate_val * sigma
    hidden = (active * up_val).astype(jnp.bfloat16)
    hid_grad = jnp.dot(flat_g, w_down, preferred_element_type=jnp.float32)
    d_gate = (hid_grad * up_val * sigma * (1.0 + gate_val * (1.0 - sigma))).astype(jnp.bfloat16)
    d_up = (hid_grad * active).astype(jnp.bfloat16)
    down_blocks = w_down.reshape(D, N_TENSOR, block_width)
    gate_blocks = w_gate.reshape(D, N_TENSOR, block_width)
    up_blocks = w_up.reshape(D, N_TENSOR, block_width)
    out_parts = block_sum(hidden.reshape(-1, N_TENSOR, block_width), down_blocks).astype(jnp.bfloat16)
    out_parts = lax.optimization_barrier(out_parts)
    out_rows = jnp.sum(out_parts.astype(jnp.float32), axis=1).astype(jnp.bfloat16)
    in_parts = (block_sum(d_gate.reshape(-1, N_TENSOR, block_width), gate_blocks)
                + block_sum(d_up.reshape(-1, N_TENSOR, block_width), up_blocks)).astype(jnp.bfloat16)
    in_parts = lax.optimization_barrier(in_parts)
    in_rows = jnp.sum(in_parts.astype(jnp.float32), axis=1).astype(jnp.bfloat16)
    group_gate = d_gate.reshape(N_DP, -1, FF)
    group_up = d_up.reshape(N_DP, -1, FF)
    group_hidden = hidden.reshape(N_DP, -1, FF)
    contract = (((0,), (0,)), ((), ()))
    gate_grad = jnp.zeros((D, FF), jnp.float32)
    up_grad = jnp.zeros((D, FF), jnp.float32)
    down_grad = jnp.zeros((D, FF), jnp.float32)
    for part_index in range(N_DP):
        term_gate = lax.dot_general(rows_x[part_index], group_gate[part_index], contract, preferred_element_type=jnp.float32)
        term_up = lax.dot_general(rows_x[part_index], group_up[part_index], contract, preferred_element_type=jnp.float32)
        term_down = lax.dot_general(rows_g[part_index], group_hidden[part_index], contract, preferred_element_type=jnp.float32)
        gate_grad = gate_grad + lax.optimization_barrier(term_gate.astype(jnp.bfloat16)).astype(jnp.float32)
        up_grad = up_grad + lax.optimization_barrier(term_up.astype(jnp.bfloat16)).astype(jnp.float32)
        down_grad = down_grad + lax.optimization_barrier(term_down.astype(jnp.bfloat16)).astype(jnp.float32)
    return (out_rows.reshape(rows_x.shape), in_rows.reshape(rows_x.shape),
            gate_grad.astype(jnp.bfloat16), up_grad.astype(jnp.bfloat16), down_grad.astype(jnp.bfloat16))


def reference(tokens, expert_ids, gate_logits, gate_weight, up_weight, down_weight, out_grad):
    slot_count = TOK_DEV // 2
    group_count = N_DP * N_EXPERT
    group_span = EXPERTS * slot_count
    total_rows = group_count * group_span
    targets = slot_targets(expert_ids, EXPERTS, slot_count, TOK_DEV)
    group_base = (jnp.arange(group_count, dtype=jnp.int32) * group_span)[:, None]
    flat_index = (targets + group_base).reshape(-1).astype(jnp.int32)
    diff = gate_logits[:, 0] - gate_logits[:, 1]
    shares = jnp.stack([jax.nn.sigmoid(diff), jax.nn.sigmoid(-diff)], axis=1)
    token_copies = jnp.repeat(tokens, 2, axis=0)
    grad_copies = (shares[:, :, None] * out_grad.astype(jnp.float32)[:, None, :]).astype(jnp.bfloat16).reshape(-1, D)
    dispatched = jnp.zeros((total_rows, D), jnp.bfloat16).at[flat_index].set(token_copies)
    grad_disp = jnp.zeros((total_rows, D), jnp.bfloat16).at[flat_index].set(grad_copies)

    def to_experts(values):
        shaped = values.reshape(N_DP, N_EXPERT, EXPERTS, slot_count, D)
        return shaped.transpose(2, 0, 1, 3, 4).reshape(EXPERTS, N_DP, N_EXPERT * slot_count, D)

    def from_experts(values):
        shaped = values.reshape(EXPERTS, N_DP, N_EXPERT, slot_count, D)
        return shaped.transpose(1, 2, 0, 3, 4).reshape(total_rows, D)

    out_all, in_all, gate_grad, up_grad, down_grad = lax.map(
        expert_pass, (to_experts(dispatched), to_experts(grad_disp), gate_weight, up_weight, down_weight))
    out_picked = from_experts(out_all)[flat_index].reshape(TOKENS, 2, D).astype(jnp.float32)
    in_picked = from_experts(in_all)[flat_index].reshape(TOKENS, 2, D).astype(jnp.float32)
    mixed = jnp.sum(shares[:, :, None] * out_picked, axis=1).astype(jnp.bfloat16)
    input_grad = jnp.sum(in_picked, axis=1).astype(jnp.bfloat16)
    weighted = jnp.einsum("td,tkd->tk", out_grad.astype(jnp.float32), out_picked, precision=lax.Precision.HIGHEST)
    logit_grad = shares * (weighted - jnp.sum(shares * weighted, axis=1, keepdims=True))
    return mixed, input_grad, logit_grad, gate_grad, up_grad, down_grad
```

```python
import functools

import jax
import jax.numpy as jnp
from jax import lax
from jax.experimental import pallas as pl
from jax.experimental.pallas import tpu as pltpu
from jax.sharding import PartitionSpec as P

MESH = pl.DeviceIdType.MESH
F32 = jnp.float32
BF16 = jnp.bfloat16
Y = 2


def dot(a, b):
    return jnp.dot(a, b, preferred_element_type=F32)


def dot_tn(a, b):
    return lax.dot_general(a, b, (((0,), (0,)), ((), ())), preferred_element_type=F32)


def dot_nt(a, b, precision=None):
    return lax.dot_general(
        a, b, (((1,), (1,)), ((), ())), precision=precision, preferred_element_type=F32
    )


def eye(n):
    rows = lax.broadcasted_iota(jnp.int32, (n, n), 0)
    cols = lax.broadcasted_iota(jnp.int32, (n, n), 1)
    return (rows == cols).astype(F32).astype(BF16)


def kernel(
    sizes,
    tok_ref,
    ids_ref,
    logit_ref,
    wg_hbm,
    wu_hbm,
    wd_hbm,
    og_ref,
    mixed_ref,
    in_grad_ref,
    logit_grad_ref,
    gate_grad_ref,
    up_grad_ref,
    down_grad_ref,
    wg,
    wu,
    wd,
    stage,
    out0,
    in0,
    xg,
    acc,
    both_sums,
    hid,
    xq,
    hq,
    plus_out,
    plus_in,
    minus_out,
    minus_in,
    pair_out,
    pair_in,
    sw_out,
    sw_in,
    sw_all,
    out4,
    in4,
    w_sem,
    s0_sem,
    r0_sem,
    sy_sem,
    ry_sem,
    sp_sem,
    rp_sem,
    sm_sem,
    rm_sem,
    xq_s,
    xq_r,
    hq_s,
    hq_r,
    tp_s,
    tp_r,
    tm_s,
    tm_r,
    pair_s,
    pair_r,
    sw_s,
    sw_r,
    swx_s,
    swx_r,
    s4_sem,
    r4_sem,
):
    n_dp, n_exp, nz, tok, feat, hidw, pad = sizes
    slot = tok // 2
    rows = n_exp * slot
    hp, hm = nz // 2, nz // 2 - 1
    planes = nz // n_dp
    d = lax.axis_index("dp")
    e = lax.axis_index("expert")
    t_me = lax.axis_index("tensor")
    z, y = t_me // Y, t_me % Y
    y_other = 1 - y
    up_to = lax.rem(z + 1, nz) * Y + y
    down_to = lax.rem(z + nz - 1, nz) * Y + y
    pair = z * Y + y_other
    strides = []
    m = 1
    while m < nz:
        strides.append(m)
        m *= 2

    def flip(m):
        return (z + m - 2 * m * (lax.rem(z // m, 2))) * Y + y

    tensor_peers = [up_to, down_to, pair] + [
        flip(m) for m in strides if m not in (1, nz - 1)
    ]
    barrier = pltpu.get_barrier_semaphore()
    for peer in tensor_peers:
        pl.semaphore_signal(barrier, inc=1, device_id={"tensor": peer}, device_id_type=MESH)
    for o in range(1, n_exp):
        pl.semaphore_signal(
            barrier, inc=1, device_id={"expert": lax.rem(e + o, n_exp)}, device_id_type=MESH
        )
    for o in range(1, n_dp):
        pl.semaphore_signal(
            barrier, inc=1, device_id={"dp": lax.rem(d + o, n_dp)}, device_id_type=MESH
        )
    loads = [
        pltpu.make_async_copy(src, dst, w_sem.at[i])
        for i, (src, dst) in enumerate(((wg_hbm, wg), (wu_hbm, wu), (wd_hbm, wd)))
    ]
    for load in loads:
        load.start()

    ids = ids_ref[...]
    id_k = (ids[:, 0:1], ids[:, 1:2])
    lanes = lax.broadcasted_iota(jnp.int32, (tok, 128), 1)
    hot = [(lanes == i).astype(F32) for i in id_k]
    later = lax.broadcasted_iota(jnp.int32, (tok, tok), 0)
    earlier = lax.broadcasted_iota(jnp.int32, (tok, tok), 1)
    before = (earlier < later).astype(F32).astype(BF16)
    count = dot(before, (hot[0] + hot[1]).astype(BF16))
    place = [jnp.sum(h * count, axis=1, keepdims=True).astype(jnp.int32) for h in hot]
    row_lane = lax.broadcasted_iota(jnp.int32, (tok, rows), 1)
    select = [
        (row_lane == i * slot + p).astype(F32).astype(BF16) for i, p in zip(id_k, place)
    ]
    logits = logit_ref[...]
    diff = logits[:, 0:1] - logits[:, 1:2]
    share = (jax.nn.sigmoid(diff), jax.nn.sigmoid(-diff))

    stage[...] = jnp.zeros_like(stage)
    out4[...] = jnp.zeros_like(out4)
    tokens = tok_ref[...]
    grads = og_ref[...].astype(F32)
    for k in range(2):
        stage[k * tok : (k + 1) * tok, 0:feat] = tokens
        stage[k * tok : (k + 1) * tok, pad : pad + feat] = (share[k] * grads).astype(BF16)
    placed = dot_tn(jnp.concatenate(select, axis=0), stage[...]).astype(BF16)
    out0[...] = placed.reshape(n_exp, slot, 2 * pad)

    pl.semaphore_wait(barrier, len(tensor_peers) + n_exp - 1 + n_dp - 1)

    def swap(src, dst, send, recv, o):
        return pltpu.make_async_remote_copy(
            src_ref=src.at[lax.rem(e + o, n_exp)],
            dst_ref=dst.at[e],
            send_sem=send.at[o - 1],
            recv_sem=recv.at[o - 1],
            device_id={"expert": lax.rem(e + o, n_exp)},
            device_id_type=MESH,
        )

    for o in range(1, n_exp):
        swap(out0, in0, s0_sem, r0_sem, o).start()
    in0[pl.ds(e, 1)] = out0[pl.ds(e, 1)]
    for o in range(1, n_exp):
        swap(out0, in0, s0_sem, r0_sem, o).wait_recv()

    unit = eye(pad)
    for a in range(2):
        arrived = in0[:, :, a * pad : (a + 1) * pad].reshape(rows, pad)
        turned = dot_nt(unit, arrived)
        xg[pl.ds(z, 1), pl.ds(y, 1), a] = turned[0:feat].astype(BF16)[None, None]

    def to_pair():
        return pltpu.make_async_remote_copy(
            src_ref=xg.at[z, y],
            dst_ref=xg.at[z, y],
            send_sem=sy_sem,
            recv_sem=ry_sem,
            device_id={"tensor": pair},
            device_id_type=MESH,
        )

    def hop(up, k, c):
        block = lax.rem(z - k + nz, nz) if up else lax.rem(z + k, nz)
        half = y if c == 0 else y_other
        return pltpu.make_async_remote_copy(
            src_ref=xg.at[block, half],
            dst_ref=xg.at[block, half],
            send_sem=(sp_sem if up else sm_sem).at[k, c],
            recv_sem=(rp_sem if up else rm_sem).at[k, c],
            device_id={"tensor": up_to if up else down_to},
            device_id_type=MESH,
        )

    def accumulate(block):
        both = xg[pl.ds(block, 1)]
        xt = both[0, :, 0].reshape(Y * feat, rows)
        gt = both[0, :, 1].reshape(Y * feat, rows)
        acc[0] += dot_tn(xt, wg[pl.ds(block, 1)][0])
        acc[1] += dot_tn(xt, wu[pl.ds(block, 1)][0])
        acc[2] += dot_tn(gt, wd[pl.ds(block, 1)][0])

    to_pair().start()
    hop(True, 0, 0).start()
    if hm > 0:
        hop(False, 0, 0).start()
    acc[...] = jnp.zeros_like(acc)
    for load in loads:
        load.wait()
    to_pair().wait_recv()
    hop(True, 0, 1).start()
    if hm > 0:
        hop(False, 0, 1).start()
    accumulate(z)

    @pl.loop(1, max(hm, 1))
    def _(k):
        for c in range(2):
            hop(True, k - 1, c).wait_recv()
            hop(True, k, c).start()
            hop(False, k - 1, c).wait_recv()
            hop(False, k, c).start()
        accumulate(lax.rem(z - k + nz, nz))
        accumulate(lax.rem(z + k, nz))

    if hm > 0:
        for c in range(2):
            hop(True, hp - 2, c).wait_recv()
            hop(True, hp - 1, c).start()
        for c in range(2):
            hop(False, hm - 1, c).wait_recv()
        accumulate(lax.rem(z - hm + nz, nz))
        accumulate(lax.rem(z + hm, nz))
    for c in range(2):
        hop(True, hp - 1, c).wait_recv()
    accumulate(lax.rem(z - hp + nz, nz))

    def quarter(o):
        peer = lax.rem(d + o, n_dp)
        return pltpu.make_async_remote_copy(
            src_ref=xg.at[pl.ds(peer * planes, planes)],
            dst_ref=xq.at[o - 1],
            send_sem=xq_s.at[o - 1],
            recv_sem=xq_r.at[o - 1],
            device_id={"dp": peer},
            device_id_type=MESH,
        )

    def factors(o):
        return pltpu.make_async_remote_copy(
            src_ref=hid,
            dst_ref=hq.at[o - 1],
            send_sem=hq_s.at[o - 1],
            recv_sem=hq_r.at[o - 1],
            device_id={"dp": lax.rem(d + o, n_dp)},
            device_id_type=MESH,
        )

    for o in range(1, n_dp):
        quarter(o).start()

    gate, lift, hid_grad = acc[0], acc[1], acc[2]
    sigma = jax.nn.sigmoid(gate)
    active = gate * sigma
    hidden = active * lift
    hid[:, 0:hidw] = hidden.astype(BF16)
    hid[:, hidw : 2 * hidw] = (
        hid_grad * lift * sigma * (1.0 + gate * (1.0 - sigma))
    ).astype(BF16)
    hid[:, 2 * hidw : 3 * hidw] = (hid_grad * active).astype(BF16)

    def own(block, a):
        if a == 0:
            return dot_nt(wd[pl.ds(block, 1)][0], hid[:, 0:hidw])
        return dot_nt(wg[pl.ds(block, 1)][0], hid[:, hidw : 2 * hidw]) + dot_nt(
            wu[pl.ds(block, 1)][0], hid[:, 2 * hidw : 3 * hidw]
        )

    def pass_on(up, k, a):
        return pltpu.make_async_remote_copy(
            src_ref=(plus_out if up else minus_out).at[k, a],
            dst_ref=(plus_in if up else minus_in).at[k, a],
            send_sem=(tp_s if up else tm_s).at[k, a],
            recv_sem=(tp_r if up else tm_r).at[k, a],
            device_id={"tensor": up_to if up else down_to},
            device_id_type=MESH,
        )

    def taken(up, k, a):
        pass_on(up, k, a).wait_recv()
        got = (plus_in if up else minus_in)[pl.ds(k, 1), a]
        return got.reshape(Y * feat, rows).astype(F32)

    def reduce_step(k, first, ways):
        for a in range(2):
            for up in ways:
                block = lax.rem(z + hp - k, nz) if up else lax.rem(z - hm + k + nz, nz)
                term = own(block, a)
                if not first:
                    term = term + taken(up, k - 1, a)
                buf = plus_out if up else minus_out
                buf[pl.ds(k, 1), a] = term.astype(BF16).reshape(1, Y, feat, rows)
                pass_on(up, k, a).start()

    def sw_copy(i, peer):
        return pltpu.make_async_remote_copy(
            src_ref=sw_out.at[i],
            dst_ref=sw_in.at[i],
            send_sem=sw_s.at[i],
            recv_sem=sw_r.at[i],
            device_id={"tensor": peer},
            device_id_type=MESH,
        )

    def sw_stage(i, m):
        sw_copy(i - 1, pair).wait_recv()
        sw_out[pl.ds(i, 1)] = sw_out[pl.ds(i - 1, 1)] + sw_in[pl.ds(i - 1, 1)]
        sw_copy(i, flip(m)).start()
        return 2 * m

    ways = (True, False) if hm > 0 else (True,)
    reduce_step(0, True, ways)
    for o in range(1, n_dp):
        factors(o).start()
    sw_out[0] = dot_nt(
        jnp.ones((8, hidw), F32), hidden * hid_grad, lax.Precision.HIGHEST
    )
    sw_copy(0, pair).start()

    n_mid = max(hm - 1, 0)
    with_sw = min(n_mid, len(strides))

    def early(k, m):
        reduce_step(k, False, ways)
        return sw_stage(k, m)

    def late(k, m):
        reduce_step(k, False, ways)
        return m

    m = lax.fori_loop(1, 1 + with_sw, early, jnp.int32(1))
    lax.fori_loop(1 + with_sw, 1 + n_mid, late, jnp.int32(1))
    for i in range(with_sw, len(strides)):
        m = sw_stage(i + 1, m)
    last = len(strides)
    sw_copy(last, pair).wait_recv()
    sw_all[pl.ds(e, 1)] = (sw_out[last] + sw_in[last])[None]

    def sw_swap(o):
        return pltpu.make_async_remote_copy(
            src_ref=sw_all.at[e],
            dst_ref=sw_all.at[e],
            send_sem=swx_s.at[o - 1],
            recv_sem=swx_r.at[o - 1],
            device_id={"expert": lax.rem(e + o, n_exp)},
            device_id_type=MESH,
        )

    for o in range(1, n_exp):
        sw_swap(o).start()
    if hm > 0:
        reduce_step(hp - 1, False, (True,))

    def halves(a):
        term = own(z, a) + taken(True, hp - 1, a)
        if hm > 0:
            term = term + taken(False, hm - 1, a)
        both_sums[a] = term.reshape(Y, feat, rows)

    def to_partner(a):
        return pltpu.make_async_remote_copy(
            src_ref=pair_out.at[a],
            dst_ref=pair_in.at[a],
            send_sem=pair_s.at[a],
            recv_sem=pair_r.at[a],
            device_id={"tensor": pair},
            device_id_type=MESH,
        )

    for a in range(2):
        halves(a)
        pair_out[a] = both_sums[a, pl.ds(y_other, 1)][0].astype(BF16)
        to_partner(a).start()
    back = eye(rows)
    for a in range(2):
        mine = both_sums[a, pl.ds(y, 1)][0]
        to_partner(a).wait_recv()
        total = (mine + pair_in[a].astype(F32)).astype(BF16)
        turned = dot_nt(back, total).astype(BF16)
        out4[:, :, a * pad : a * pad + feat] = turned.reshape(n_exp, slot, feat)
    for o in range(1, n_exp):
        swap(out4, in4, s4_sem, r4_sem, o).start()
    in4[pl.ds(e, 1)] = out4[pl.ds(e, 1)]

    for o in range(1, n_dp):
        quarter(o).wait_recv()
        factors(o).wait_recv()

    @pl.loop(0, planes)
    def _(p):
        both = [xg[pl.ds(d * planes + p, 1)][0]] + [
            xq[o, pl.ds(p, 1)][0] for o in range(n_dp - 1)
        ]
        parts = [hid] + [hq.at[o] for o in range(n_dp - 1)]
        here = pl.ds(pl.multiple_of(p * Y * feat, Y * feat), Y * feat)
        for ref, a, i in (
            (gate_grad_ref, 0, 1),
            (up_grad_ref, 0, 2),
            (down_grad_ref, 1, 0),
        ):
            total = None
            for b, h in zip(both, parts):
                term = dot(b[:, a].reshape(Y * feat, rows), h[:, i * hidw : (i + 1) * hidw])
                total = term if total is None else total + term
            ref[here, :] = total.astype(BF16)

    for o in range(1, n_exp):
        swap(out4, in4, s4_sem, r4_sem, o).wait_recv()
        sw_swap(o).wait_recv()
    came = in4[...].reshape(rows, 2 * pad)
    picked = [dot(s, came) for s in select]
    mixed_ref[...] = (
        share[0] * picked[0][:, 0:feat] + share[1] * picked[1][:, 0:feat]
    ).astype(BF16)
    in_grad_ref[...] = (
        picked[0][:, pad : pad + feat] + picked[1][:, pad : pad + feat]
    ).astype(BF16)
    sw_lane = lax.broadcasted_iota(jnp.int32, (tok, rows), 1)
    sw = []
    for k in range(2):
        line = jnp.zeros((tok, rows), F32)
        for i in range(n_exp):
            line = line + hot[k][:, i : i + 1] * jnp.concatenate([sw_all[i]] * (tok // 8), axis=0)
        here = sw_lane == e * slot + place[k]
        sw.append(jnp.sum(jnp.where(here, line, 0.0), axis=1, keepdims=True))
    first = share[1] * sw[0] - share[0] * sw[1]
    column = lax.broadcasted_iota(jnp.int32, (tok, 2), 1)
    logit_grad_ref[...] = jnp.where(column == 0, first, -first)

    for o in range(1, n_exp):
        swap(out0, in0, s0_sem, r0_sem, o).wait_send()
        swap(out4, in4, s4_sem, r4_sem, o).wait_send()
        sw_swap(o).wait_send()
    to_pair().wait_send()
    for o in range(1, n_dp):
        quarter(o).wait_send()
        factors(o).wait_send()
    for i in range(len(strides) + 1):
        sw_copy(i, pair).wait_send()
    for a in range(2):
        to_partner(a).wait_send()

    @pl.loop(0, hp)
    def _(k):
        for c in range(2):
            hop(True, k, c).wait_send()
            pass_on(True, k, c).wait_send()

    @pl.loop(0, hm)
    def _(k):
        for c in range(2):
            hop(False, k, c).wait_send()
            pass_on(False, k, c).wait_send()


def solution(mesh):
    n_dp, n_exp, n_t = mesh.shape["dp"], mesh.shape["expert"], mesh.shape["tensor"]
    nz = n_t // Y

    def on_device(tokens, expert_ids, gate_logits, gate_weight, up_weight, down_weight, out_grad):
        tok, feat = tokens.shape
        hidw = gate_weight.shape[2]
        slot = tok // 2
        rows = n_exp * slot
        hp, hm = nz // 2, nz // 2 - 1
        hmb = max(hm, 1)
        planes = nz // n_dp
        pad = -(-feat // 128) * 128
        stages = nz.bit_length()
        width = feat * n_t // n_dp
        vmem = pl.BlockSpec(memory_space=pltpu.VMEM)
        hbm = pl.BlockSpec(memory_space=pl.ANY)
        dma = pltpu.SemaphoreType.DMA
        weights = [w.reshape(nz, Y * feat, hidw) for w in (gate_weight, up_weight, down_weight)]
        grad = jax.ShapeDtypeStruct((width, hidw), BF16)
        outs = pl.pallas_call(
            functools.partial(kernel, (n_dp, n_exp, nz, tok, feat, hidw, pad)),
            out_shape=(
                jax.ShapeDtypeStruct((tok, feat), BF16),
                jax.ShapeDtypeStruct((tok, feat), BF16),
                jax.ShapeDtypeStruct((tok, 2), F32),
                grad,
                grad,
                grad,
            ),
            in_specs=[vmem, vmem, vmem, hbm, hbm, hbm, vmem],
            out_specs=[vmem] * 6,
            scratch_shapes=[
                pltpu.VMEM((nz, Y * feat, hidw), BF16),
                pltpu.VMEM((nz, Y * feat, hidw), BF16),
                pltpu.VMEM((nz, Y * feat, hidw), BF16),
                pltpu.VMEM((2 * tok, 2 * pad), BF16),
                pltpu.VMEM((n_exp, slot, 2 * pad), BF16),
                pltpu.VMEM((n_exp, slot, 2 * pad), BF16),
                pltpu.VMEM((nz, Y, 2, feat, rows), BF16),
                pltpu.VMEM((3, rows, hidw), F32),
                pltpu.VMEM((2, Y, feat, rows), F32),
                pltpu.VMEM((rows, 3 * hidw), BF16),
                pltpu.VMEM((n_dp - 1, planes, Y, 2, feat, rows), BF16),
                pltpu.VMEM((n_dp - 1, rows, 3 * hidw), BF16),
                pltpu.VMEM((hp, 2, Y, feat, rows), BF16),
                pltpu.VMEM((hp, 2, Y, feat, rows), BF16),
                pltpu.VMEM((hmb, 2, Y, feat, rows), BF16),
                pltpu.VMEM((hmb, 2, Y, feat, rows), BF16),
                pltpu.VMEM((2, feat, rows), BF16),
                pltpu.VMEM((2, feat, rows), BF16),
                pltpu.VMEM((stages, 8, rows), F32),
                pltpu.VMEM((stages, 8, rows), F32),
                pltpu.VMEM((n_exp, 8, rows), F32),
                pltpu.VMEM((n_exp, slot, 2 * pad), BF16),
                pltpu.VMEM((n_exp, slot, 2 * pad), BF16),
                dma((3,)),
                dma((n_exp - 1,)),
                dma((n_exp - 1,)),
                dma,
                dma,
                dma((hp, 2)),
                dma((hp, 2)),
                dma((hmb, 2)),
                dma((hmb, 2)),
                dma((n_dp - 1,)),
                dma((n_dp - 1,)),
                dma((n_dp - 1,)),
                dma((n_dp - 1,)),
                dma((hp, 2)),
                dma((hp, 2)),
                dma((hmb, 2)),
                dma((hmb, 2)),
                dma((2,)),
                dma((2,)),
                dma((stages,)),
                dma((stages,)),
                dma((n_exp - 1,)),
                dma((n_exp - 1,)),
                dma((n_exp - 1,)),
                dma((n_exp - 1,)),
            ],
            compiler_params=pltpu.CompilerParams(
                collective_id=0, has_side_effects=True, vmem_limit_bytes=40 * 1024 * 1024
            ),
        )(tokens, expert_ids, gate_logits, *weights, out_grad)
        mixed, in_grad, logit_grad, gate_grad, up_grad, down_grad = outs
        return mixed, in_grad, logit_grad, gate_grad[None], up_grad[None], down_grad[None]

    return jax.shard_map(
        on_device,
        mesh=mesh,
        in_specs=(
            P(("dp", "expert"), "tensor"),
            P(("dp", "expert"), None),
            P(("dp", "expert"), None),
            P("expert", None, "tensor"),
            P("expert", None, "tensor"),
            P("expert", None, "tensor"),
            P(("dp", "expert"), "tensor"),
        ),
        out_specs=(
            P(("dp", "expert"), "tensor"),
            P(("dp", "expert"), "tensor"),
            P(("dp", "expert"), None),
            P("expert", "dp", "tensor"),
            P("expert", "dp", "tensor"),
            P("expert", "dp", "tensor"),
        ),
        check_vma=False,
    )
```

```python
import functools

import jax
import jax.numpy as jnp
from jax import lax
from jax.experimental import pallas as pl
from jax.experimental.pallas import tpu as pltpu
from jax.sharding import PartitionSpec as P

MESH = pl.DeviceIdType.MESH
F32 = jnp.float32
BF16 = jnp.bfloat16
Y = 2


def dot(a, b):
    return jnp.dot(a, b, preferred_element_type=F32)


def dot_tn(a, b):
    return lax.dot_general(a, b, (((0,), (0,)), ((), ())), preferred_element_type=F32)


def dot_nt(a, b, precision=None):
    return lax.dot_general(
        a, b, (((1,), (1,)), ((), ())), precision=precision, preferred_element_type=F32
    )


def eye(n):
    rows = lax.broadcasted_iota(jnp.int32, (n, n), 0)
    cols = lax.broadcasted_iota(jnp.int32, (n, n), 1)
    return (rows == cols).astype(F32).astype(BF16)


def kernel(
    sizes,
    tok_hbm,
    ids_hbm,
    logit_hbm,
    wg_hbm,
    wu_hbm,
    wd_hbm,
    og_hbm,
    mixed_hbm,
    in_grad_hbm,
    logit_grad_hbm,
    gate_grad_hbm,
    up_grad_hbm,
    down_grad_hbm,
    tok_ref,
    ids_ref,
    logit_ref,
    og_ref,
    mixed_ref,
    in_grad_ref,
    logit_grad_ref,
    grads_ref,
    wg,
    wu,
    wd,
    stage,
    out0,
    in0,
    xg,
    acc,
    hid,
    xq,
    hq,
    terms,
    pair_out,
    pair_in,
    z_out,
    z_in,
    sw_q,
    sw_r,
    sw_y,
    sw_all,
    out4,
    in4,
    load_sem,
    store_sem,
    s0_sem,
    r0_sem,
    sy_sem,
    ry_sem,
    sg_sem,
    rg_sem,
    xq_s,
    xq_r,
    hq_s,
    hq_r,
    sp_sem,
    rp_sem,
    sz_sem,
    rz_sem,
    swq_s,
    swq_r,
    swr_s,
    swr_r,
    swy_s,
    swy_r,
    swx_s,
    swx_r,
    s4_sem,
    r4_sem,
):
    n_dp, n_exp, nz, tok, feat, hidw, pad = sizes
    slot = tok // 2
    rows = n_exp * slot
    half_ring = nz // 2
    groups = nz // 4
    planes = nz // n_dp
    d = lax.axis_index("dp")
    e = lax.axis_index("expert")
    t_me = lax.axis_index("tensor")
    z, y = t_me // Y, t_me % Y
    y_other = 1 - y

    def at_z(off):
        return lax.rem(z + (off + nz), nz)

    def device(off):
        return {"tensor": at_z(off) * Y + y}

    pair = {"tensor": z * Y + y_other}

    z_peers = [1, -1, 2] + ([-2] if nz > 4 else [])
    z_peers += [4 * k for k in range(1, groups) if nz > 4]
    peers = [device(off) for off in z_peers] + [pair]
    peers += [{"expert": lax.rem(e + o, n_exp)} for o in range(1, n_exp)]
    peers += [{"dp": lax.rem(d + o, n_dp)} for o in range(1, n_dp)]
    barrier = pltpu.get_barrier_semaphore()
    for peer in peers:
        pl.semaphore_signal(barrier, inc=1, device_id=peer, device_id_type=MESH)

    loads = [
        pltpu.make_async_copy(src, dst, load_sem.at[i])
        for i, (src, dst) in enumerate(
            (
                (ids_hbm, ids_ref),
                (logit_hbm, logit_ref),
                (tok_hbm, tok_ref),
                (og_hbm, og_ref),
                (wg_hbm, wg),
                (wu_hbm, wu),
                (wd_hbm, wd),
            )
        )
    ]
    for load in loads:
        load.start()

    def remote(src, dst, send, recv, peer):
        return pltpu.make_async_remote_copy(
            src_ref=src,
            dst_ref=dst,
            send_sem=send,
            recv_sem=recv,
            device_id=peer,
            device_id_type=MESH,
        )

    stage[...] = jnp.zeros_like(stage)
    out4[...] = jnp.zeros_like(out4)
    acc[...] = jnp.zeros_like(acc)
    later = lax.broadcasted_iota(jnp.int32, (tok, tok), 0)
    earlier = lax.broadcasted_iota(jnp.int32, (tok, tok), 1)
    before = (earlier < later).astype(F32).astype(BF16)
    lanes = lax.broadcasted_iota(jnp.int32, (tok, 128), 1)
    row_lane = lax.broadcasted_iota(jnp.int32, (tok, rows), 1)

    def column(line):
        return jnp.sum(jnp.where(later == earlier, line, 0), axis=1, keepdims=True)

    for load in loads[:2]:
        load.wait()
    ids = ids_ref[...].astype(F32)
    logits = logit_ref[...]
    id_k = [column(ids[k : k + 1, :]).astype(jnp.int32) for k in range(2)]
    hot = [(lanes == i).astype(F32) for i in id_k]
    count = dot(before, (hot[0] + hot[1]).astype(BF16))
    place = [jnp.sum(h * count, axis=1, keepdims=True).astype(jnp.int32) for h in hot]
    select = [
        (row_lane == i * slot + p).astype(F32).astype(BF16) for i, p in zip(id_k, place)
    ]
    diff = column(logits[0:1, :] - logits[1:2, :])
    share = (jax.nn.sigmoid(diff), jax.nn.sigmoid(-diff))

    for load in loads[2:4]:
        load.wait()
    tokens = tok_ref[...]
    grads = og_ref[...].astype(F32)
    for k in range(2):
        stage[k * tok : (k + 1) * tok, 0:feat] = tokens
        stage[k * tok : (k + 1) * tok, pad : pad + feat] = (share[k] * grads).astype(BF16)
    placed = dot_tn(jnp.concatenate(select, axis=0), stage[...]).astype(BF16)
    out0[...] = placed.reshape(n_exp, slot, 2 * pad)

    pl.semaphore_wait(barrier, len(peers))

    def swap(src, dst, send, recv, o):
        to = lax.rem(e + o, n_exp)
        return remote(src.at[to], dst.at[e], send.at[o - 1], recv.at[o - 1], {"expert": to})

    for o in range(1, n_exp):
        swap(out0, in0, s0_sem, r0_sem, o).start()
    in0[pl.ds(e, 1)] = out0[pl.ds(e, 1)]
    for o in range(1, n_exp):
        swap(out0, in0, s0_sem, r0_sem, o).wait_recv()

    unit = eye(pad)
    for a in range(2):
        arrived = in0[:, :, a * pad : (a + 1) * pad].reshape(rows, pad)
        turned = dot_nt(unit, arrived)
        xg[pl.ds(z, 1), pl.ds(y, 1), a] = turned[0:feat].astype(BF16)[None, None]

    def step(kind, i):
        off, to, half = {
            "chain_up": (-2 * i, 2, y),
            "chain_down": (2 * i, -2, y),
            "near_up": (-2 * i, 1, y),
            "near_down": (2 * i, -1, y),
            "both_down": (2 * i, -1, y_other),
        }[kind]
        n = ("chain_up", "chain_down", "near_up", "near_down", "both_down").index(kind)
        ref = xg.at[at_z(off), half]
        return remote(ref, ref, sg_sem.at[n, i], rg_sem.at[n, i], device(to))

    def across(off):
        ref = xg.at[at_z(off), y]
        return remote(ref, ref, sy_sem.at[off % nz], ry_sem.at[off % nz], pair)

    relayed = [2 * i + 1 for i in range(groups - 1)]

    def quarter(o, p):
        peer = lax.rem(d + o, n_dp)
        return remote(
            xg.at[peer * planes + p],
            xq.at[o - 1, p],
            xq_s.at[o - 1, p],
            xq_r.at[o - 1, p],
            {"dp": peer},
        )

    def complete(off):
        if off in relayed:
            step("both_down", (off - 1) // 2).wait_recv()
        else:
            across(off).wait_recv()
            if off >= 0 and off % 2 == 0 and off // 2 < groups - 1:
                step("both_down", off // 2).start()

    def accumulate(block):
        both = xg[pl.ds(block, 1)]
        xt = both[0, :, 0].reshape(Y * feat, rows)
        gt = both[0, :, 1].reshape(Y * feat, rows)
        acc[0] += dot_tn(xt, wg[pl.ds(block, 1)][0])
        acc[1] += dot_tn(xt, wu[pl.ds(block, 1)][0])
        acc[2] += dot_tn(gt, wd[pl.ds(block, 1)][0])

    def forward(block):
        peer, p = block // planes, lax.rem(block, planes)
        o = lax.rem(peer - d + n_dp, n_dp)

        @pl.when(o > 0)
        def _():
            remote(
                xg.at[block],
                xq.at[o - 1, p],
                xq_s.at[o - 1, p],
                xq_r.at[o - 1, p],
                {"dp": peer},
            ).start()

    def plane_group(i):
        if i == 0:
            return [0]
        offs = [-2 * i, 2 * i, -(2 * i - 1), 2 * i - 1]
        if i == groups:
            offs.remove(2 * i)
        return offs

    def use(i):
        offs = plane_group(i)
        for off in offs:
            complete(off)
        if i == 0:
            accumulate(z)
            forward(z)
            return

        @pl.loop(0, len(offs))
        def _(j):
            at = j + (j > 0).astype(jnp.int32) if i == groups else j
            off = (2 * lax.rem(at, 2) - 1) * (2 * i - at // 2)
            block = lax.rem(z + off + nz, nz)
            accumulate(block)
            forward(block)

    step("chain_up", 0).start()
    if groups > 1:
        step("chain_down", 0).start()
    across(0).start()
    step("near_up", 0).start()
    step("near_down", 0).start()
    for load in loads[4:]:
        load.wait()
    for i in range(1, groups + 1):
        step("chain_up", i - 1).wait_recv()
        if i < groups:
            step("chain_up", i).start()
            step("near_up", i).start()
            step("chain_down", i - 1).wait_recv()
            if i < groups - 1:
                step("chain_down", i).start()
            step("near_down", i).start()
        for off in plane_group(i):
            if off == -(2 * i - 1):
                step("near_up", i - 1).wait_recv()
            if off == 2 * i - 1:
                step("near_down", i - 1).wait_recv()
            if off not in relayed:
                across(off).start()
        use(i - 1)
    use(groups)

    def factors(o):
        return remote(
            hid, hq.at[o - 1], hq_s.at[o - 1], hq_r.at[o - 1], {"dp": lax.rem(d + o, n_dp)}
        )

    gate, lift, hid_grad = acc[0], acc[1], acc[2]
    sigma = jax.nn.sigmoid(gate)
    active = gate * sigma
    hidden = active * lift
    hid[:, 0:hidw] = hidden.astype(BF16)
    hid[:, hidw : 2 * hidw] = (
        hid_grad * lift * sigma * (1.0 + gate * (1.0 - sigma))
    ).astype(BF16)
    hid[:, 2 * hidw : 3 * hidw] = (hid_grad * active).astype(BF16)

    def own(block, a):
        if a == 0:
            return dot_nt(wd[pl.ds(block, 1)][0], hid[:, 0:hidw])
        return dot_nt(wg[pl.ds(block, 1)][0], hid[:, hidw : 2 * hidw]) + dot_nt(
            wu[pl.ds(block, 1)][0], hid[:, 2 * hidw : 3 * hidw]
        )

    UP, NEAR_DOWN, NEAR_UP, DOWN = range(4)
    sends_to = (2, -1, 1, -2)

    def target(g, j):
        return (
            half_ring - 2 * g,
            -(half_ring - 1) + 2 * g,
            half_ring - 1 - 2 * g,
            -(half_ring - 2) + 2 * g,
        )[j]

    def to_pair(n):
        return remote(pair_out.at[n], pair_in.at[n], sp_sem.at[n], rp_sem.at[n], pair)

    def along(j, g):
        return remote(
            z_out.at[j, g], z_in.at[j, g], sz_sem.at[j, g], rz_sem.at[j, g], device(sends_to[j])
        )

    def prepare(g):
        for j in (NEAR_DOWN, NEAR_UP, UP, DOWN):
            n = 4 * g + j
            block = at_z(target(g, j))
            for a in range(2):
                terms[n, a] = own(block, a).reshape(Y, feat, rows)
                pair_out[n, a] = terms[n, a, pl.ds(y_other, 1)][0].astype(BF16)
            to_pair(n).start()

    def settle(g, j, extra, send):
        n = 4 * g + j
        to_pair(n).wait_recv()
        for kind, i in extra:
            along(kind, i).wait_recv()
        totals = []
        for a in range(2):
            total = terms[n, a, pl.ds(y, 1)][0] + pair_in[n, a].astype(F32)
            for kind, i in extra:
                total = total + z_in[kind, i, a].astype(F32)
            if send:
                z_out[j, g, a] = total.astype(BF16)
            totals.append(total)
        if send:
            along(j, g).start()
        return totals

    prepare(0)
    for o in range(1, n_dp):
        factors(o).start()

    quad, place4 = z // 4, lax.rem(z, 4)

    def sw_quads(k):
        return remote(
            sw_q.at[quad], sw_q.at[quad], swq_s.at[k - 1], swq_r.at[k - 1], device(4 * k)
        )

    def sw_near(k):
        return remote(
            sw_r.at[place4], sw_r.at[place4], swr_s.at[k], swr_r.at[k], device((1, -1, -2)[k])
        )

    def sw_pair():
        return remote(sw_y.at[y], sw_y.at[y], swy_s, swy_r, pair)

    def sw_swap(o):
        return remote(
            sw_all.at[e],
            sw_all.at[e],
            swx_s.at[o - 1],
            swx_r.at[o - 1],
            {"expert": lax.rem(e + o, n_exp)},
        )

    line = dot_nt(jnp.ones((8, hidw), F32), hidden * hid_grad, lax.Precision.HIGHEST)
    sw_q[pl.ds(quad, 1)] = line[None]
    for k in range(1, groups):
        sw_quads(k).start()

    def sw_first():
        for k in range(1, groups):
            sw_quads(k).wait_recv()
        total = sw_q[0]
        for i in range(1, groups):
            total = total + sw_q[i]
        sw_r[pl.ds(place4, 1)] = total[None]
        for k in range(3):
            sw_near(k).start()

    def sw_second():
        for k in range(3):
            sw_near(k).wait_recv()
        sw_y[pl.ds(y, 1)] = (((sw_r[0] + sw_r[1]) + sw_r[2]) + sw_r[3])[None]
        sw_pair().start()

    def sw_third():
        sw_pair().wait_recv()
        sw_all[pl.ds(e, 1)] = (sw_y[0] + sw_y[1])[None]
        for o in range(1, n_exp):
            sw_swap(o).start()

    sw_stages = [sw_first, sw_second, sw_third]
    for g in range(groups):
        if g + 1 < groups:
            prepare(g + 1)
        settle(g, NEAR_DOWN, [], True)
        settle(g, NEAR_UP, [], True)
        settle(g, UP, [(UP, g - 1), (NEAR_UP, g - 1)] if g > 0 else [], True)
        extra = [(NEAR_DOWN, g)] + ([(DOWN, g - 1)] if g > 0 else [])
        if g < groups - 1:
            settle(g, DOWN, extra, True)
            if g > 0:
                sw_stages.pop(0)()
        else:
            totals = settle(g, DOWN, extra + [(UP, g), (NEAR_UP, g)], False)

    back = eye(rows)
    for a in range(2):
        turned = dot_nt(back, totals[a].astype(BF16)).astype(BF16)
        out4[:, :, a * pad : a * pad + feat] = turned.reshape(n_exp, slot, feat)
    for o in range(1, n_exp):
        swap(out4, in4, s4_sem, r4_sem, o).start()
    in4[pl.ds(e, 1)] = out4[pl.ds(e, 1)]
    for sw_stage in sw_stages:
        sw_stage()

    for o in range(1, n_dp):
        for p in range(planes):
            quarter(o, p).wait_recv()
        factors(o).wait_recv()

    @pl.loop(0, planes)
    def _(p):
        both = [xg[pl.ds(d * planes + p, 1)][0]] + [
            xq[o, pl.ds(p, 1)][0] for o in range(n_dp - 1)
        ]
        parts = [hid] + [hq.at[o] for o in range(n_dp - 1)]
        here = pl.ds(pl.multiple_of(p * Y * feat, Y * feat), Y * feat)
        for n, a, i in ((0, 0, 1), (1, 0, 2), (2, 1, 0)):
            total = None
            for b, h in zip(both, parts):
                term = dot(b[:, a].reshape(Y * feat, rows), h[:, i * hidw : (i + 1) * hidw])
                total = term if total is None else total + term
            grads_ref[n, here, :] = total.astype(BF16)

    stores = [
        pltpu.make_async_copy(src, dst, store_sem.at[i])
        for i, (src, dst) in enumerate(
            (
                (grads_ref.at[0], gate_grad_hbm),
                (grads_ref.at[1], up_grad_hbm),
                (grads_ref.at[2], down_grad_hbm),
                (mixed_ref, mixed_hbm),
                (in_grad_ref, in_grad_hbm),
                (logit_grad_ref, logit_grad_hbm),
            )
        )
    ]
    for store in stores[:3]:
        store.start()

    for o in range(1, n_exp):
        swap(out4, in4, s4_sem, r4_sem, o).wait_recv()
    came = in4[...].reshape(rows, 2 * pad)
    picked = [dot(s, came) for s in select]
    mixed_ref[...] = (
        share[0] * picked[0][:, 0:feat] + share[1] * picked[1][:, 0:feat]
    ).astype(BF16)
    in_grad_ref[...] = (
        picked[0][:, pad : pad + feat] + picked[1][:, pad : pad + feat]
    ).astype(BF16)
    for store in stores[3:5]:
        store.start()
    for o in range(1, n_exp):
        sw_swap(o).wait_recv()
    sw = []
    for k in range(2):
        line = jnp.zeros((tok, rows), F32)
        for i in range(n_exp):
            line = line + hot[k][:, i : i + 1] * jnp.concatenate([sw_all[i]] * (tok // 8), axis=0)
        here = row_lane == e * slot + place[k]
        sw.append(jnp.sum(jnp.where(here, line, 0.0), axis=1, keepdims=True))
    first = jnp.sum(
        jnp.where(later == earlier, share[1] * sw[0] - share[0] * sw[1], 0.0),
        axis=0,
        keepdims=True,
    )
    which = lax.broadcasted_iota(jnp.int32, (2, tok), 0)
    logit_grad_ref[...] = jnp.where(which == 0, first, -first)
    stores[5].start()

    for o in range(1, n_exp):
        swap(out0, in0, s0_sem, r0_sem, o).wait_send()
        swap(out4, in4, s4_sem, r4_sem, o).wait_send()
        sw_swap(o).wait_send()
    for i in range(groups):
        step("chain_up", i).wait_send()
        step("near_up", i).wait_send()
        step("near_down", i).wait_send()
        if i < groups - 1:
            step("chain_down", i).wait_send()
            step("both_down", i).wait_send()
        for j in (NEAR_DOWN, NEAR_UP, UP, DOWN):
            to_pair(4 * i + j).wait_send()
            if j != DOWN or i < groups - 1:
                along(j, i).wait_send()
    for off in range(nz):
        if off not in relayed:
            across(off).wait_send()
    for o in range(1, n_dp):
        for p in range(planes):
            quarter(o, p).wait_send()
        factors(o).wait_send()
    for k in range(1, groups):
        sw_quads(k).wait_send()
    for k in range(3):
        sw_near(k).wait_send()
    sw_pair().wait_send()
    for store in stores:
        store.wait()


def hand_over(*refs):
    count = (len(refs) - 2) // 3
    sources, results, held = refs[:count], refs[count : 2 * count], refs[2 * count : 3 * count]
    in_sem, out_sem = refs[-2:]
    ins = [pltpu.make_async_copy(sources[i], held[i], in_sem.at[i]) for i in range(count)]
    outs = [pltpu.make_async_copy(held[i], results[i], out_sem.at[i]) for i in range(count)]
    for copy in ins:
        copy.start()
    for before, after in zip(ins, outs):
        before.wait()
        after.start()
    for copy in outs:
        copy.wait()


def solution(mesh):
    n_dp, n_exp, n_t = mesh.shape["dp"], mesh.shape["expert"], mesh.shape["tensor"]
    nz = n_t // Y

    def on_device(tokens, expert_ids, gate_logits, gate_weight, up_weight, down_weight, out_grad):
        tok, feat = tokens.shape
        hidw = gate_weight.shape[2]
        slot = tok // 2
        rows = n_exp * slot
        groups = nz // 4
        planes = nz // n_dp
        pad = -(-feat // 128) * 128
        width = feat * n_t // n_dp
        hbm = pl.BlockSpec(memory_space=pl.ANY)
        dma = pltpu.SemaphoreType.DMA
        weights = [w.reshape(nz, Y * feat, hidw) for w in (gate_weight, up_weight, down_weight)]
        grad = jax.ShapeDtypeStruct((width, hidw), BF16)
        shapes = (
            jax.ShapeDtypeStruct((tok, feat), BF16),
            jax.ShapeDtypeStruct((tok, feat), BF16),
            jax.ShapeDtypeStruct((2, tok), F32),
            grad,
            grad,
            grad,
        )
        block = (2, feat, rows)
        outs = pl.pallas_call(
            functools.partial(kernel, (n_dp, n_exp, nz, tok, feat, hidw, pad)),
            out_shape=shapes,
            in_specs=[hbm] * 7,
            out_specs=[hbm] * 6,
            scratch_shapes=[
                pltpu.VMEM((tok, feat), BF16),
                pltpu.VMEM((2, tok), jnp.int32),
                pltpu.VMEM((2, tok), F32),
                pltpu.VMEM((tok, feat), BF16),
                pltpu.VMEM((tok, feat), BF16),
                pltpu.VMEM((tok, feat), BF16),
                pltpu.VMEM((2, tok), F32),
                pltpu.VMEM((3, width, hidw), BF16),
                pltpu.VMEM((nz, Y * feat, hidw), BF16),
                pltpu.VMEM((nz, Y * feat, hidw), BF16),
                pltpu.VMEM((nz, Y * feat, hidw), BF16),
                pltpu.VMEM((2 * tok, 2 * pad), BF16),
                pltpu.VMEM((n_exp, slot, 2 * pad), BF16),
                pltpu.VMEM((n_exp, slot, 2 * pad), BF16),
                pltpu.VMEM((nz, Y) + block, BF16),
                pltpu.VMEM((3, rows, hidw), F32),
                pltpu.VMEM((rows, 3 * hidw), BF16),
                pltpu.VMEM((n_dp - 1, planes, Y) + block, BF16),
                pltpu.VMEM((n_dp - 1, rows, 3 * hidw), BF16),
                pltpu.VMEM((nz, 2, Y, feat, rows), F32),
                pltpu.VMEM((nz,) + block, BF16),
                pltpu.VMEM((nz,) + block, BF16),
                pltpu.VMEM((4, groups) + block, BF16),
                pltpu.VMEM((4, groups) + block, BF16),
                pltpu.VMEM((groups, 8, rows), F32),
                pltpu.VMEM((4, 8, rows), F32),
                pltpu.VMEM((Y, 8, rows), F32),
                pltpu.VMEM((n_exp, 8, rows), F32),
                pltpu.VMEM((n_exp, slot, 2 * pad), BF16),
                pltpu.VMEM((n_exp, slot, 2 * pad), BF16),
                dma((7,)),
                dma((6,)),
                dma((n_exp - 1,)),
                dma((n_exp - 1,)),
                dma((nz,)),
                dma((nz,)),
                dma((5, groups)),
                dma((5, groups)),
                dma((n_dp - 1, planes)),
                dma((n_dp - 1, planes)),
                dma((n_dp - 1,)),
                dma((n_dp - 1,)),
                dma((nz,)),
                dma((nz,)),
                dma((4, groups)),
                dma((4, groups)),
                dma((max(groups - 1, 1),)),
                dma((max(groups - 1, 1),)),
                dma((3,)),
                dma((3,)),
                dma,
                dma,
                dma((n_exp - 1,)),
                dma((n_exp - 1,)),
                dma((n_exp - 1,)),
                dma((n_exp - 1,)),
            ],
            compiler_params=pltpu.CompilerParams(
                collective_id=0, has_side_effects=True, vmem_limit_bytes=60 * 1024 * 1024
            ),
        )(tokens, expert_ids.T, gate_logits.T, *weights, out_grad)
        mixed, in_grad, logit_grad, gate_grad, up_grad, down_grad = pl.pallas_call(
            hand_over,
            out_shape=shapes,
            in_specs=[hbm] * 6,
            out_specs=[hbm] * 6,
            scratch_shapes=[pltpu.VMEM(out.shape, out.dtype) for out in shapes]
            + [dma((6,)), dma((6,))],
            compiler_params=pltpu.CompilerParams(vmem_limit_bytes=60 * 1024 * 1024),
        )(*outs)
        return mixed, in_grad, logit_grad.T, gate_grad[None], up_grad[None], down_grad[None]

    return jax.shard_map(
        on_device,
        mesh=mesh,
        in_specs=(
            P(("dp", "expert"), "tensor"),
            P(("dp", "expert"), None),
            P(("dp", "expert"), None),
            P("expert", None, "tensor"),
            P("expert", None, "tensor"),
            P("expert", None, "tensor"),
            P(("dp", "expert"), "tensor"),
        ),
        out_specs=(
            P(("dp", "expert"), "tensor"),
            P(("dp", "expert"), "tensor"),
            P(("dp", "expert"), None),
            P("expert", "dp", "tensor"),
            P("expert", "dp", "tensor"),
            P("expert", "dp", "tensor"),
        ),
        check_vma=False,
    )
```

```python
import functools

import jax
import jax.numpy as jnp
from jax import lax
from jax.experimental import pallas as pl
from jax.experimental.pallas import tpu as pltpu
from jax.sharding import PartitionSpec as P

MESH = pl.DeviceIdType.MESH
F32 = jnp.float32
BF16 = jnp.bfloat16
Y = 2


def dot(a, b):
    return jnp.dot(a, b, preferred_element_type=F32)


def dot_tn(a, b):
    return lax.dot_general(a, b, (((0,), (0,)), ((), ())), preferred_element_type=F32)


def dot_nt(a, b, precision=None):
    return lax.dot_general(
        a, b, (((1,), (1,)), ((), ())), precision=precision, preferred_element_type=F32
    )


def eye(n):
    rows = lax.broadcasted_iota(jnp.int32, (n, n), 0)
    cols = lax.broadcasted_iota(jnp.int32, (n, n), 1)
    return (rows == cols).astype(F32).astype(BF16)


def tree(nz):
    groups = nz // 4
    parent, levels, doubled = {}, [[0]], []
    for i in range(groups):
        up, down = [2 * i + 2, 2 * i + 1], [-2 * i - 1]
        if i < groups - 1:
            down.insert(0, -2 * i - 2)
        if i > 0 and i >= groups - 2:
            doubled.append(-2 * i - 1)
        if i > 0 and i == groups - 1:
            doubled.append(2 * i + 1)
        parent.update({k: 2 * i for k in up})
        parent.update({k: -2 * i for k in down})
        levels.append([k for pair in zip(up, down) for k in pair] + up[len(down) :])
    return parent, levels, tuple(doubled)


def kernel(
    sizes,
    tok_hbm,
    ids_hbm,
    logit_hbm,
    wg_hbm,
    wu_hbm,
    wd_hbm,
    og_hbm,
    mixed_hbm,
    in_grad_hbm,
    logit_grad_hbm,
    gate_grad_hbm,
    up_grad_hbm,
    down_grad_hbm,
    tok_ref,
    ids_ref,
    logit_ref,
    og_ref,
    mixed_ref,
    in_grad_ref,
    logit_grad_ref,
    grads_ref,
    wg,
    wu,
    wd,
    stage,
    out0,
    in0,
    xg,
    acc,
    hid,
    xq,
    hq,
    terms,
    pair_out,
    pair_in,
    z_out,
    z_in,
    both_out,
    both_in,
    sw_z,
    sw_y,
    sw_all,
    out4,
    in4,
    load_sem,
    store_sem,
    s0_sem,
    r0_sem,
    sy_sem,
    ry_sem,
    sg_sem,
    rg_sem,
    sb_sem,
    rb_sem,
    xq_s,
    xq_r,
    hq_s,
    hq_r,
    sp_sem,
    rp_sem,
    sz_sem,
    rz_sem,
    so_sem,
    ro_sem,
    swz_s,
    swz_r,
    swy_s,
    swy_r,
    swx_s,
    swx_r,
    s4_sem,
    r4_sem,
):
    n_dp, n_exp, nz, tok, feat, hidw, pad = sizes
    slot = tok // 2
    rows = n_exp * slot
    planes = nz // n_dp
    parent, levels, doubled = tree(nz)
    others = [k for level in levels[1:] for k in level]
    children = {
        k: sorted((c for c in others if parent[c] == k), key=lambda c: -abs(c - k))
        for k in [0] + others
    }
    d = lax.axis_index("dp")
    e = lax.axis_index("expert")
    t_me = lax.axis_index("tensor")
    z, y = t_me // Y, t_me % Y
    y_other = 1 - y

    def at_z(off):
        return lax.rem(z + (off + nz), nz)

    def device(off):
        return {"tensor": at_z(off) * Y + y}

    pair = {"tensor": z * Y + y_other}

    hops = {k - parent[k] for k in others}
    z_peers = sorted({h % nz for h in hops} | {-h % nz for h in hops})
    peers = [device(off) for off in z_peers] + [pair]
    peers += [{"expert": lax.rem(e + o, n_exp)} for o in range(1, n_exp)]
    peers += [{"dp": lax.rem(d + o, n_dp)} for o in range(1, n_dp)]
    barrier = pltpu.get_barrier_semaphore()
    for peer in peers:
        pl.semaphore_signal(barrier, inc=1, device_id=peer, device_id_type=MESH)

    loads = [
        pltpu.make_async_copy(src, dst, load_sem.at[i])
        for i, (src, dst) in enumerate(
            (
                (ids_hbm, ids_ref),
                (logit_hbm, logit_ref),
                (tok_hbm, tok_ref),
                (og_hbm, og_ref),
                (wg_hbm, wg),
                (wu_hbm, wu),
                (wd_hbm, wd),
            )
        )
    ]
    for load in loads:
        load.start()

    def remote(src, dst, send, recv, peer):
        return pltpu.make_async_remote_copy(
            src_ref=src,
            dst_ref=dst,
            send_sem=send,
            recv_sem=recv,
            device_id=peer,
            device_id_type=MESH,
        )

    stage[...] = jnp.zeros_like(stage)
    out4[...] = jnp.zeros_like(out4)
    acc[...] = jnp.zeros_like(acc)
    later = lax.broadcasted_iota(jnp.int32, (tok, tok), 0)
    earlier = lax.broadcasted_iota(jnp.int32, (tok, tok), 1)
    before = (earlier < later).astype(F32).astype(BF16)
    lanes = lax.broadcasted_iota(jnp.int32, (tok, 128), 1)
    row_lane = lax.broadcasted_iota(jnp.int32, (tok, rows), 1)

    def column(line):
        return jnp.sum(jnp.where(later == earlier, line, 0), axis=1, keepdims=True)

    for load in loads[:2]:
        load.wait()
    ids = ids_ref[...].astype(F32)
    logits = logit_ref[...]
    id_k = [column(ids[k : k + 1, :]).astype(jnp.int32) for k in range(2)]
    hot = [(lanes == i).astype(F32) for i in id_k]
    count = dot(before, (hot[0] + hot[1]).astype(BF16))
    place = [jnp.sum(h * count, axis=1, keepdims=True).astype(jnp.int32) for h in hot]
    select = [
        (row_lane == i * slot + p).astype(F32).astype(BF16) for i, p in zip(id_k, place)
    ]
    diff = column(logits[0:1, :] - logits[1:2, :])
    share = (jax.nn.sigmoid(diff), jax.nn.sigmoid(-diff))

    for load in loads[2:4]:
        load.wait()
    tokens = tok_ref[...]
    grads = og_ref[...].astype(F32)
    for k in range(2):
        stage[k * tok : (k + 1) * tok, 0:feat] = tokens
        stage[k * tok : (k + 1) * tok, pad : pad + feat] = (share[k] * grads).astype(BF16)
    placed = dot_tn(jnp.concatenate(select, axis=0), stage[...]).astype(BF16)
    out0[...] = placed.reshape(n_exp, slot, 2 * pad)

    pl.semaphore_wait(barrier, len(peers))

    def swap(src, dst, send, recv, o):
        to = lax.rem(e + o, n_exp)
        return remote(src.at[to], dst.at[e], send, recv.at[o - 1], {"expert": to})

    for o in range(1, n_exp):
        swap(out0, in0, s0_sem, r0_sem, o).start()
    in0[pl.ds(e, 1)] = out0[pl.ds(e, 1)]
    for o in range(1, n_exp):
        swap(out0, in0, s0_sem, r0_sem, o).wait_recv()

    unit = eye(pad)
    for a in range(2):
        arrived = in0[:, :, a * pad : (a + 1) * pad].reshape(rows, pad)
        turned = dot_nt(unit, arrived)
        xg[pl.ds(z, 1), pl.ds(y, 1), a] = turned[0:feat].astype(BF16)[None, None]

    def deliver(c):
        ref = xg.at[at_z(-parent[c]), y]
        return remote(ref, ref, sg_sem, rg_sem.at[c % nz], device(c - parent[c]))

    def deliver_other(c):
        ref = xg.at[at_z(-parent[c]), y_other]
        n = doubled.index(c)
        return remote(ref, ref, sb_sem, rb_sem.at[n], device(c - parent[c]))

    def arrive(c):
        ref = xg.at[at_z(-c), y]
        remote(ref, ref, sg_sem, rg_sem.at[c % nz], device(c - parent[c])).wait_recv()

    def arrive_other(c):
        ref = xg.at[at_z(-c), y_other]
        n = doubled.index(c)
        remote(ref, ref, sb_sem, rb_sem.at[n], device(c - parent[c])).wait_recv()

    def across(k):
        ref = xg.at[at_z(-k), y]
        return remote(ref, ref, sy_sem, ry_sem.at[k % nz], pair)

    def quarter(o, p):
        peer = lax.rem(d + o, n_dp)
        return remote(
            xg.at[peer * planes + p],
            xq.at[o - 1, p],
            xq_s,
            xq_r.at[o - 1, p],
            {"dp": peer},
        )

    def complete(k):
        if k in doubled:
            arrive_other(k)
        else:
            across(k).wait_recv()
            for c in children[k]:
                if c in doubled:
                    deliver_other(c).start()

    def accumulate(block):
        both = xg[pl.ds(block, 1)]
        xt = both[0, :, 0].reshape(Y * feat, rows)
        gt = both[0, :, 1].reshape(Y * feat, rows)
        acc[0] += dot_tn(xt, wg[pl.ds(block, 1)][0])
        acc[1] += dot_tn(xt, wu[pl.ds(block, 1)][0])
        acc[2] += dot_tn(gt, wd[pl.ds(block, 1)][0])

    def forward(block):
        peer, p = block // planes, lax.rem(block, planes)
        o = lax.rem(peer - d + n_dp, n_dp)

        @pl.when(o > 0)
        def _():
            remote(
                xg.at[block],
                xq.at[o - 1, p],
                xq_s,
                xq_r.at[o - 1, p],
                {"dp": peer},
            ).start()

    early = sorted({parent[c] for c in doubled})

    def use(level):
        for k in levels[level]:
            if k not in early:
                complete(k)
            accumulate(at_z(-k))
            forward(at_z(-k))

    for level, offsets in enumerate(levels):
        for k in offsets:
            if level > 0:
                arrive(k)
            far = [c for c in children[k] if abs(c - k) > 1]
            for c in far:
                deliver(c).start()
            if k not in doubled:
                across(k).start()
            for c in children[k]:
                if c not in far:
                    deliver(c).start()
        if level == 0:
            for load in loads[4:]:
                load.wait()
        else:
            use(level - 1)
        for k in offsets:
            if k in early:
                complete(k)
    use(len(levels) - 1)

    def factors(o):
        return remote(
            hid, hq.at[o - 1], hq_s, hq_r.at[o - 1], {"dp": lax.rem(d + o, n_dp)}
        )

    gate, lift, hid_grad = acc[0], acc[1], acc[2]
    sigma = jax.nn.sigmoid(gate)
    active = gate * sigma
    hidden = active * lift
    hid[:, 0:hidw] = hidden.astype(BF16)
    hid[:, hidw : 2 * hidw] = (
        hid_grad * lift * sigma * (1.0 + gate * (1.0 - sigma))
    ).astype(BF16)
    hid[:, 2 * hidw : 3 * hidw] = (hid_grad * active).astype(BF16)

    def own(block, a):
        if a == 0:
            return dot_nt(wd[pl.ds(block, 1)][0], hid[:, 0:hidw])
        return dot_nt(wg[pl.ds(block, 1)][0], hid[:, hidw : 2 * hidw]) + dot_nt(
            wu[pl.ds(block, 1)][0], hid[:, 2 * hidw : 3 * hidw]
        )

    def to_pair(k):
        n = k % nz
        return remote(pair_out.at[n], pair_in.at[n], sp_sem, rp_sem.at[n], pair)

    def along(k):
        n = k % nz
        return remote(
            z_out.at[n], z_in.at[n], sz_sem, rz_sem.at[n], device(parent[k] - k)
        )

    def along_other(k):
        n = doubled.index(k)
        return remote(
            both_out.at[n], both_in.at[n], so_sem, ro_sem.at[n], device(parent[k] - k)
        )

    def prepare(k):
        n = k % nz
        for a in range(2):
            terms[n, a] = own(at_z(-k), a).reshape(Y, feat, rows)
            if k in doubled:
                z_out[n, a] = terms[n, a, pl.ds(y, 1)][0].astype(BF16)
                both_out[doubled.index(k), a] = terms[n, a, pl.ds(y_other, 1)][0].astype(BF16)
        if k in doubled:
            along(k).start()
            along_other(k).start()

    def hand(k):
        n = k % nz
        added = [c for c in children[k] if c in doubled]
        for c in added:
            along_other(c).wait_recv()
        for a in range(2):
            theirs = terms[n, a, pl.ds(y_other, 1)][0]
            for c in added:
                theirs = theirs + both_in[doubled.index(c), a].astype(F32)
            pair_out[n, a] = theirs.astype(BF16)
        to_pair(k).start()

    def settle(k):
        n = k % nz
        to_pair(k).wait_recv()
        for c in children[k]:
            along(c).wait_recv()
        totals = []
        for a in range(2):
            total = terms[n, a, pl.ds(y, 1)][0] + pair_in[n, a].astype(F32)
            for c in children[k]:
                total = total + z_in[c % nz, a].astype(F32)
            if k != 0:
                z_out[n, a] = total.astype(BF16)
            totals.append(total)
        if k != 0:
            along(k).start()
        return totals

    def terms_of(level):
        order = levels[level][::-1] if level == 0 else levels[level]
        waits = [k for k in order if k in early]
        for k in order:
            prepare(k)
            if k not in doubled and k not in waits:
                hand(k)
        for k in waits:
            hand(k)

    last = len(levels) - 1
    terms_of(last)
    for o in range(1, n_dp):
        factors(o).start()

    def sw_send(c):
        ref = sw_z.at[at_z(-parent[c])]
        return remote(ref, ref, swz_s, swz_r.at[c % nz], device(c - parent[c]))

    def sw_arrive(c):
        ref = sw_z.at[at_z(-c)]
        remote(ref, ref, swz_s, swz_r.at[c % nz], device(c - parent[c])).wait_recv()

    def sw_pair():
        return remote(sw_y.at[y], sw_y.at[y], swy_s, swy_r, pair)

    def sw_swap(o):
        return remote(
            sw_all.at[e],
            sw_all.at[e],
            swx_s,
            swx_r.at[o - 1],
            {"expert": lax.rem(e + o, n_exp)},
        )

    line = dot_nt(jnp.ones((8, hidw), F32), hidden * hid_grad, lax.Precision.HIGHEST)
    sw_z[pl.ds(z, 1)] = line[None]

    def sw_level(level):
        for k in levels[level]:
            if level > 0:
                sw_arrive(k)
            for c in children[k]:
                sw_send(c).start()

    def sw_planes():
        total = sw_z[0]
        for i in range(1, nz):
            total = total + sw_z[i]
        sw_y[pl.ds(y, 1)] = total[None]
        sw_pair().start()

    def sw_experts():
        sw_pair().wait_recv()
        sw_all[pl.ds(e, 1)] = (sw_y[0] + sw_y[1])[None]
        for o in range(1, n_exp):
            sw_swap(o).start()

    sw_level(0)
    if last > 1:
        terms_of(last - 1)
    for k in levels[last]:
        if k not in doubled:
            settle(k)
    sw_level(1)
    for level in range(last - 1, 0, -1):
        terms_of(level - 1)
        for k in levels[level]:
            if not children[k] and k not in doubled:
                settle(k)
        if level == 1:
            sw_level(last)
            sw_planes()
        for k in levels[level]:
            if children[k]:
                settle(k)
        if level > 1:
            sw_level(last - level + 1)
    if last == 1:
        terms_of(0)
        sw_planes()
    totals = settle(0)

    back = eye(rows)
    for a in range(2):
        turned = dot_nt(back, totals[a].astype(BF16)).astype(BF16)
        out4[:, :, a * pad : a * pad + feat] = turned.reshape(n_exp, slot, feat)
    for o in range(1, n_exp):
        swap(out4, in4, s4_sem, r4_sem, o).start()
    in4[pl.ds(e, 1)] = out4[pl.ds(e, 1)]
    sw_experts()

    for o in range(1, n_dp):
        for p in range(planes):
            quarter(o, p).wait_recv()
        factors(o).wait_recv()

    @pl.loop(0, planes)
    def _(p):
        both = [xg[pl.ds(d * planes + p, 1)][0]] + [
            xq[o, pl.ds(p, 1)][0] for o in range(n_dp - 1)
        ]
        parts = [hid] + [hq.at[o] for o in range(n_dp - 1)]
        here = pl.ds(pl.multiple_of(p * Y * feat, Y * feat), Y * feat)
        for n, a, i in ((0, 0, 1), (1, 0, 2), (2, 1, 0)):
            total = None
            for b, h in zip(both, parts):
                term = dot(b[:, a].reshape(Y * feat, rows), h[:, i * hidw : (i + 1) * hidw])
                total = term if total is None else total + term
            grads_ref[n, here, :] = total.astype(BF16)

    stores = [
        pltpu.make_async_copy(src, dst, store_sem.at[i])
        for i, (src, dst) in enumerate(
            (
                (grads_ref.at[0], gate_grad_hbm),
                (grads_ref.at[1], up_grad_hbm),
                (grads_ref.at[2], down_grad_hbm),
                (mixed_ref, mixed_hbm),
                (in_grad_ref, in_grad_hbm),
                (logit_grad_ref, logit_grad_hbm),
            )
        )
    ]
    for store in stores[:3]:
        store.start()

    def sent(ref, sem):
        remote(ref, ref, sem, rg_sem.at[0], pair).wait_send()

    count, singles = len(others), nz - len(doubled)
    sent(out0.at[pl.ds(0, n_exp - 1)], s0_sem)
    sent(xg.at[pl.ds(0, count), 0], sg_sem)
    sent(xg.at[pl.ds(0, singles), 0], sy_sem)
    sent(z_out.at[pl.ds(0, count)], sz_sem)
    sent(pair_out.at[pl.ds(0, singles)], sp_sem)
    if doubled:
        sent(xg.at[pl.ds(0, len(doubled)), 0], sb_sem)
        sent(both_out.at[pl.ds(0, len(doubled))], so_sem)
    sent(sw_z.at[pl.ds(0, count)], swz_s)
    sent(xq, xq_s)
    sent(hq, hq_s)
    sw_pair().wait_send()

    for o in range(1, n_exp):
        swap(out4, in4, s4_sem, r4_sem, o).wait_recv()
    came = in4[...].reshape(rows, 2 * pad)
    picked = [dot(s, came) for s in select]
    mixed_ref[...] = (
        share[0] * picked[0][:, 0:feat] + share[1] * picked[1][:, 0:feat]
    ).astype(BF16)
    in_grad_ref[...] = (
        picked[0][:, pad : pad + feat] + picked[1][:, pad : pad + feat]
    ).astype(BF16)
    for store in stores[3:5]:
        store.start()
    for o in range(1, n_exp):
        sw_swap(o).wait_recv()
    sw = []
    for k in range(2):
        line = jnp.zeros((tok, rows), F32)
        for i in range(n_exp):
            line = line + hot[k][:, i : i + 1] * jnp.concatenate([sw_all[i]] * (tok // 8), axis=0)
        here = row_lane == e * slot + place[k]
        sw.append(jnp.sum(jnp.where(here, line, 0.0), axis=1, keepdims=True))
    first = jnp.sum(
        jnp.where(later == earlier, share[1] * sw[0] - share[0] * sw[1], 0.0),
        axis=0,
        keepdims=True,
    )
    which = lax.broadcasted_iota(jnp.int32, (2, tok), 0)
    logit_grad_ref[...] = jnp.where(which == 0, first, -first)
    stores[5].start()

    sent(out4.at[pl.ds(0, n_exp - 1)], s4_sem)
    sent(sw_all.at[pl.ds(0, n_exp - 1)], swx_s)
    for store in stores:
        store.wait()


def hand_over(*refs):
    count = (len(refs) - 2) // 3
    sources, results, held = refs[:count], refs[count : 2 * count], refs[2 * count : 3 * count]
    in_sem, out_sem = refs[-2:]
    ins = [pltpu.make_async_copy(sources[i], held[i], in_sem.at[i]) for i in range(count)]
    outs = [pltpu.make_async_copy(held[i], results[i], out_sem.at[i]) for i in range(count)]
    for copy in ins:
        copy.start()
    for before, after in zip(ins, outs):
        before.wait()
        after.start()
    for copy in outs:
        copy.wait()


def solution(mesh):
    n_dp, n_exp, n_t = mesh.shape["dp"], mesh.shape["expert"], mesh.shape["tensor"]
    nz = n_t // Y

    def on_device(tokens, expert_ids, gate_logits, gate_weight, up_weight, down_weight, out_grad):
        tok, feat = tokens.shape
        hidw = gate_weight.shape[2]
        slot = tok // 2
        rows = n_exp * slot
        planes = nz // n_dp
        pad = -(-feat // 128) * 128
        width = feat * n_t // n_dp
        hbm = pl.BlockSpec(memory_space=pl.ANY)
        dma = pltpu.SemaphoreType.DMA
        weights = [w.reshape(nz, Y * feat, hidw) for w in (gate_weight, up_weight, down_weight)]
        grad = jax.ShapeDtypeStruct((width, hidw), BF16)
        shapes = (
            jax.ShapeDtypeStruct((tok, feat), BF16),
            jax.ShapeDtypeStruct((tok, feat), BF16),
            jax.ShapeDtypeStruct((2, tok), F32),
            grad,
            grad,
            grad,
        )
        block = (2, feat, rows)
        outs = pl.pallas_call(
            functools.partial(kernel, (n_dp, n_exp, nz, tok, feat, hidw, pad)),
            out_shape=shapes,
            in_specs=[hbm] * 7,
            out_specs=[hbm] * 6,
            scratch_shapes=[
                pltpu.VMEM((tok, feat), BF16),
                pltpu.VMEM((2, tok), jnp.int32),
                pltpu.VMEM((2, tok), F32),
                pltpu.VMEM((tok, feat), BF16),
                pltpu.VMEM((tok, feat), BF16),
                pltpu.VMEM((tok, feat), BF16),
                pltpu.VMEM((2, tok), F32),
                pltpu.VMEM((3, width, hidw), BF16),
                pltpu.VMEM((nz, Y * feat, hidw), BF16),
                pltpu.VMEM((nz, Y * feat, hidw), BF16),
                pltpu.VMEM((nz, Y * feat, hidw), BF16),
                pltpu.VMEM((2 * tok, 2 * pad), BF16),
                pltpu.VMEM((n_exp, slot, 2 * pad), BF16),
                pltpu.VMEM((n_exp, slot, 2 * pad), BF16),
                pltpu.VMEM((nz, Y) + block, BF16),
                pltpu.VMEM((3, rows, hidw), F32),
                pltpu.VMEM((rows, 3 * hidw), BF16),
                pltpu.VMEM((n_dp - 1, planes, Y) + block, BF16),
                pltpu.VMEM((n_dp - 1, rows, 3 * hidw), BF16),
                pltpu.VMEM((nz, 2, Y, feat, rows), F32),
                pltpu.VMEM((nz,) + block, BF16),
                pltpu.VMEM((nz,) + block, BF16),
                pltpu.VMEM((nz,) + block, BF16),
                pltpu.VMEM((nz,) + block, BF16),
                pltpu.VMEM((3,) + block, BF16),
                pltpu.VMEM((3,) + block, BF16),
                pltpu.VMEM((nz, 8, rows), F32),
                pltpu.VMEM((Y, 8, rows), F32),
                pltpu.VMEM((n_exp, 8, rows), F32),
                pltpu.VMEM((n_exp, slot, 2 * pad), BF16),
                pltpu.VMEM((n_exp, slot, 2 * pad), BF16),
                dma((7,)),
                dma((6,)),
                dma,
                dma((n_exp - 1,)),
                dma,
                dma((nz,)),
                dma,
                dma((nz,)),
                dma,
                dma((3,)),
                dma,
                dma((n_dp - 1, planes)),
                dma,
                dma((n_dp - 1,)),
                dma,
                dma((nz,)),
                dma,
                dma((nz,)),
                dma,
                dma((3,)),
                dma,
                dma((nz,)),
                dma,
                dma,
                dma,
                dma((n_exp - 1,)),
                dma,
                dma((n_exp - 1,)),
            ],
            compiler_params=pltpu.CompilerParams(
                collective_id=0, has_side_effects=True, vmem_limit_bytes=60 * 1024 * 1024
            ),
        )(tokens, expert_ids.T, gate_logits.T, *weights, out_grad)
        mixed, in_grad, logit_grad, gate_grad, up_grad, down_grad = pl.pallas_call(
            hand_over,
            out_shape=shapes,
            in_specs=[hbm] * 6,
            out_specs=[hbm] * 6,
            scratch_shapes=[pltpu.VMEM(out.shape, out.dtype) for out in shapes]
            + [dma((6,)), dma((6,))],
            compiler_params=pltpu.CompilerParams(vmem_limit_bytes=60 * 1024 * 1024),
        )(*outs)
        return mixed, in_grad, logit_grad.T, gate_grad[None], up_grad[None], down_grad[None]

    return jax.shard_map(
        on_device,
        mesh=mesh,
        in_specs=(
            P(("dp", "expert"), "tensor"),
            P(("dp", "expert"), None),
            P(("dp", "expert"), None),
            P("expert", None, "tensor"),
            P("expert", None, "tensor"),
            P("expert", None, "tensor"),
            P(("dp", "expert"), "tensor"),
        ),
        out_specs=(
            P(("dp", "expert"), "tensor"),
            P(("dp", "expert"), "tensor"),
            P(("dp", "expert"), None),
            P("expert", "dp", "tensor"),
            P("expert", "dp", "tensor"),
            P("expert", "dp", "tensor"),
        ),
        check_vma=False,
    )
```

```python
import functools

import jax
import jax.numpy as jnp
from jax import lax
from jax.experimental import pallas as pl
from jax.experimental.pallas import tpu as pltpu
from jax.sharding import PartitionSpec as P

MESH = pl.DeviceIdType.MESH
F32 = jnp.float32
BF16 = jnp.bfloat16
Y = 2


def dot(a, b):
    return jnp.dot(a, b, preferred_element_type=F32)


def dot_tn(a, b):
    return lax.dot_general(a, b, (((0,), (0,)), ((), ())), preferred_element_type=F32)


def dot_nt(a, b, precision=None):
    return lax.dot_general(
        a, b, (((1,), (1,)), ((), ())), precision=precision, preferred_element_type=F32
    )


def eye(n):
    rows = lax.broadcasted_iota(jnp.int32, (n, n), 0)
    cols = lax.broadcasted_iota(jnp.int32, (n, n), 1)
    return (rows == cols).astype(F32).astype(BF16)


def tree(nz):
    groups = nz // 4
    parent, levels = {}, [[0]]
    for i in range(groups):
        up, down = [2 * i + 2, 2 * i + 1], [-2 * i - 1]
        if i < groups - 1:
            down.insert(0, -2 * i - 2)
        parent.update({k: 2 * i for k in up})
        parent.update({k: -2 * i for k in down})
        levels.append([k for pair in zip(up, down) for k in pair] + up[len(down) :])
    end = 2 * groups
    doubled = [k for k in (3 - end, end - 1, 1 - end) if groups > 1 and parent[k] != 0]
    return parent, levels, doubled, {end: 2 - end, end - 1: end - 2, 1 - end: 2 - end}


def kernel(
    sizes,
    tok_hbm,
    ids_hbm,
    logit_hbm,
    wg_hbm,
    wu_hbm,
    wd_hbm,
    og_hbm,
    mixed_hbm,
    in_grad_hbm,
    logit_grad_hbm,
    gate_grad_hbm,
    up_grad_hbm,
    down_grad_hbm,
    tok_ref,
    ids_ref,
    logit_ref,
    og_ref,
    mixed_ref,
    in_grad_ref,
    logit_grad_ref,
    grads_ref,
    wg,
    wu,
    wd,
    stage,
    out0,
    in0,
    xg,
    acc,
    hid,
    xq,
    hq,
    terms,
    pair_out,
    pair_in,
    z_out,
    z_in,
    both_out,
    both_in,
    sw_z,
    sw_y,
    sw_all,
    out4,
    in4,
    load_sem,
    store_sem,
    s0_sem,
    r0_sem,
    sy_sem,
    ry_sem,
    sg_sem,
    rg_sem,
    sb_sem,
    rb_sem,
    xq_s,
    xq_r,
    hq_s,
    hq_r,
    sp_sem,
    rp_sem,
    sz_sem,
    rz_sem,
    so_sem,
    ro_sem,
    swz_s,
    swz_r,
    swy_s,
    swy_r,
    swx_s,
    swx_r,
    s4_sem,
    r4_sem,
):
    n_dp, n_exp, nz, tok, feat, hidw, pad = sizes
    slot = tok // 2
    rows = n_exp * slot
    planes = nz // n_dp
    parent, levels, doubled, crossing = tree(nz)
    others = [k for level in levels[1:] for k in level]
    cross = list(crossing)
    children = {
        k: sorted((c for c in others if parent[c] == k), key=lambda c: -abs(c - k))
        for k in [0] + others
    }
    d = lax.axis_index("dp")
    e = lax.axis_index("expert")
    t_me = lax.axis_index("tensor")
    z, y = t_me // Y, t_me % Y
    y_other = 1 - y

    def at_z(off):
        return lax.rem(z + (off + nz), nz)

    def device(off, other=False):
        return {"tensor": at_z(off) * Y + (y_other if other else y)}

    def crossed(c):
        hop = c - crossing[c]
        return hop - nz if hop > 2 else hop

    pair = {"tensor": z * Y + y_other}

    hops = {k - parent[k] for k in others}
    z_peers = sorted({h % nz for h in hops} | {-h % nz for h in hops})
    peers = [device(off) for off in z_peers] + [pair]
    peers += [device(off, True) for off in z_peers]
    peers += [{"expert": lax.rem(e + o, n_exp)} for o in range(1, n_exp)]
    peers += [{"dp": lax.rem(d + o, n_dp)} for o in range(1, n_dp)]
    barrier = pltpu.get_barrier_semaphore()
    for peer in peers:
        pl.semaphore_signal(barrier, inc=1, device_id=peer, device_id_type=MESH)

    loads = [
        pltpu.make_async_copy(src, dst, load_sem.at[i])
        for i, (src, dst) in enumerate(
            (
                (ids_hbm, ids_ref),
                (logit_hbm, logit_ref),
                (tok_hbm, tok_ref),
                (og_hbm, og_ref),
                (wg_hbm, wg),
                (wu_hbm, wu),
                (wd_hbm, wd),
            )
        )
    ]
    for load in loads:
        load.start()

    def remote(src, dst, send, recv, peer):
        return pltpu.make_async_remote_copy(
            src_ref=src,
            dst_ref=dst,
            send_sem=send,
            recv_sem=recv,
            device_id=peer,
            device_id_type=MESH,
        )

    stage[...] = jnp.zeros_like(stage)
    out4[...] = jnp.zeros_like(out4)
    acc[...] = jnp.zeros_like(acc)
    later = lax.broadcasted_iota(jnp.int32, (tok, tok), 0)
    earlier = lax.broadcasted_iota(jnp.int32, (tok, tok), 1)
    before = (earlier < later).astype(F32).astype(BF16)
    lanes = lax.broadcasted_iota(jnp.int32, (tok, 128), 1)
    row_lane = lax.broadcasted_iota(jnp.int32, (tok, rows), 1)

    def column(line):
        return jnp.sum(jnp.where(later == earlier, line, 0), axis=1, keepdims=True)

    for load in loads[:2]:
        load.wait()
    ids = ids_ref[...].astype(F32)
    logits = logit_ref[...]
    id_k = [column(ids[k : k + 1, :]).astype(jnp.int32) for k in range(2)]
    hot = [(lanes == i).astype(F32) for i in id_k]
    count = dot(before, (hot[0] + hot[1]).astype(BF16))
    place = [jnp.sum(h * count, axis=1, keepdims=True).astype(jnp.int32) for h in hot]
    select = [
        (row_lane == i * slot + p).astype(F32).astype(BF16) for i, p in zip(id_k, place)
    ]
    diff = column(logits[0:1, :] - logits[1:2, :])
    share = (jax.nn.sigmoid(diff), jax.nn.sigmoid(-diff))

    for load in loads[2:4]:
        load.wait()
    tokens = tok_ref[...]
    grads = og_ref[...].astype(F32)
    for k in range(2):
        stage[k * tok : (k + 1) * tok, 0:feat] = tokens
        stage[k * tok : (k + 1) * tok, pad : pad + feat] = (share[k] * grads).astype(BF16)
    placed = dot_tn(jnp.concatenate(select, axis=0), stage[...]).astype(BF16)
    out0[...] = placed.reshape(n_exp, slot, 2 * pad)

    pl.semaphore_wait(barrier, len(peers))

    def swap(src, dst, send, recv, o):
        to = lax.rem(e + o, n_exp)
        return remote(src.at[to], dst.at[e], send, recv, {"expert": to})

    for o in range(1, n_exp):
        swap(out0, in0, s0_sem, r0_sem, o).start()
    in0[pl.ds(e, 1)] = out0[pl.ds(e, 1)]
    arrived = in0.at[pl.ds(0, n_exp - 1)]
    remote(arrived, arrived, s0_sem, r0_sem, pair).wait_recv()

    unit = eye(pad)
    for a in range(2):
        arrived = in0[:, :, a * pad : (a + 1) * pad].reshape(rows, pad)
        turned = dot_nt(unit, arrived)
        xg[pl.ds(z, 1), pl.ds(y, 1), a] = turned[0:feat].astype(BF16)[None, None]

    def deliver(c):
        ref = xg.at[at_z(-parent[c]), y]
        return remote(ref, ref, sg_sem, rg_sem.at[c % nz], device(c - parent[c]))

    def deliver_other(c):
        ref = xg.at[at_z(-parent[c]), y_other]
        n = doubled.index(c)
        return remote(ref, ref, sb_sem, rb_sem.at[n], device(c - parent[c]))

    def arrive(c):
        ref = xg.at[at_z(-c), y]
        remote(ref, ref, sg_sem, rg_sem.at[c % nz], device(c - parent[c])).wait_recv()

    def arrive_other(c):
        ref = xg.at[at_z(-c), y_other]
        n = doubled.index(c)
        remote(ref, ref, sb_sem, rb_sem.at[n], device(c - parent[c])).wait_recv()

    def across(k):
        ref = xg.at[at_z(-k), y]
        return remote(ref, ref, sy_sem, ry_sem.at[k % nz], pair)

    def complete(k):
        if k in doubled:
            arrive_other(k)
        else:
            across(k).wait_recv()
            for c in children[k]:
                if c in doubled:
                    deliver_other(c).start()

    def accumulate(block):
        both = xg[pl.ds(block, 1)]
        xt = both[0, :, 0].reshape(Y * feat, rows)
        gt = both[0, :, 1].reshape(Y * feat, rows)
        acc[0] += dot_tn(xt, wg[pl.ds(block, 1)][0])
        acc[1] += dot_tn(xt, wu[pl.ds(block, 1)][0])
        acc[2] += dot_tn(gt, wd[pl.ds(block, 1)][0])

    def forward(block):
        peer, p = block // planes, lax.rem(block, planes)
        o = lax.rem(peer - d + n_dp, n_dp)

        @pl.when(o > 0)
        def _():
            remote(
                xg.at[block],
                xq.at[o - 1, p],
                xq_s,
                xq_r,
                {"dp": peer},
            ).start()

    early = sorted({parent[c] for c in doubled})

    def use(level):
        for k in levels[level]:
            if k not in early:
                complete(k)
            accumulate(at_z(-k))
            forward(at_z(-k))

    last = len(levels) - 1
    for level, offsets in enumerate(levels):
        for k in offsets:
            if level > 0:
                arrive(k)
            for c in children[k]:
                if abs(c - k) > 1:
                    deliver(c).start()
            if k not in doubled:
                across(k).start()
            for c in children[k]:
                if abs(c - k) == 1:
                    deliver(c).start()
        if level == 0:
            for load in loads[4:]:
                load.wait()
        else:
            use(level - 1)
        for k in offsets:
            if k in early:
                complete(k)
    use(last)

    def factors(o):
        return remote(
            hid, hq.at[o - 1], hq_s, hq_r, {"dp": lax.rem(d + o, n_dp)}
        )

    gate, lift, hid_grad = acc[0], acc[1], acc[2]
    sigma = jax.nn.sigmoid(gate)
    active = gate * sigma
    hidden = active * lift
    hid[:, 0:hidw] = hidden.astype(BF16)
    hid[:, hidw : 2 * hidw] = (
        hid_grad * lift * sigma * (1.0 + gate * (1.0 - sigma))
    ).astype(BF16)
    hid[:, 2 * hidw : 3 * hidw] = (hid_grad * active).astype(BF16)

    def own(block, a):
        if a == 0:
            return dot_nt(wd[pl.ds(block, 1)][0], hid[:, 0:hidw])
        return dot_nt(wg[pl.ds(block, 1)][0], hid[:, hidw : 2 * hidw]) + dot_nt(
            wu[pl.ds(block, 1)][0], hid[:, 2 * hidw : 3 * hidw]
        )

    def to_pair(k):
        n = k % nz
        return remote(pair_out.at[n], pair_in.at[n], sp_sem, rp_sem.at[n], pair)

    def along(k):
        n = k % nz
        return remote(
            z_out.at[n], z_in.at[n], sz_sem, rz_sem.at[n], device(parent[k] - k)
        )

    def along_across(k):
        n = cross.index(k)
        return remote(
            both_out.at[n], both_in.at[n], so_sem, ro_sem.at[n], device(-crossed(k), True)
        )

    def prepare(k):
        n = k % nz
        for a in range(2):
            terms[n, a] = own(at_z(-k), a).reshape(Y, feat, rows)
            if k in crossing:
                z_out[n, a] = terms[n, a, pl.ds(y, 1)][0].astype(BF16)
                both_out[cross.index(k), a] = terms[n, a, pl.ds(y_other, 1)][0].astype(BF16)
        if k in crossing:
            along(k).start()
            along_across(k).start()

    def hand(k):
        n = k % nz
        for a in range(2):
            pair_out[n, a] = terms[n, a, pl.ds(y_other, 1)][0].astype(BF16)
        to_pair(k).start()

    def settle(k):
        n = k % nz
        to_pair(k).wait_recv()
        for c in children[k]:
            along(c).wait_recv()
        over = [c for c in cross if crossing[c] == k]
        for c in over:
            along_across(c).wait_recv()
        totals = []
        for a in range(2):
            total = terms[n, a, pl.ds(y, 1)][0] + pair_in[n, a].astype(F32)
            for c in children[k]:
                total = total + z_in[c % nz, a].astype(F32)
            for c in over:
                total = total + both_in[cross.index(c), a].astype(F32)
            if k != 0:
                z_out[n, a] = total.astype(BF16)
            totals.append(total)
        if k != 0:
            along(k).start()
        return totals

    chain = [[k for k in level if children[k]] for level in levels]
    near = [[k for k in level if not children[k]] for level in levels]
    for k in levels[last]:
        prepare(k)
    for o in range(1, n_dp):
        factors(o).start()

    def sw_send(off):
        ref = sw_z.at[z]
        return remote(ref, ref, swz_s, swz_r, device(off))

    def sw_pair():
        return remote(sw_y.at[y], sw_y.at[y], swy_s, swy_r, pair)

    def sw_swap(o):
        return remote(
            sw_all.at[e],
            sw_all.at[e],
            swx_s,
            swx_r,
            {"expert": lax.rem(e + o, n_exp)},
        )

    line = dot_nt(jnp.ones((8, hidw), F32), hidden * hid_grad, lax.Precision.HIGHEST)
    sw_z[pl.ds(z, 1)] = line[None]

    def sw_begin():
        for off in range(1, nz):
            sw_send(off).start()

    def sw_planes():
        arrived = sw_z.at[pl.ds(0, nz - 1)]
        remote(arrived, arrived, swz_s, swz_r, pair).wait_recv()
        total = sw_z[0]
        for i in range(1, nz):
            total = total + sw_z[i]
        sw_y[pl.ds(y, 1)] = total[None]
        sw_pair().start()

    def sw_experts():
        sw_pair().wait_recv()
        sw_all[pl.ds(e, 1)] = (sw_y[0] + sw_y[1])[None]
        for o in range(1, n_exp):
            sw_swap(o).start()

    for k in levels[last - 1]:
        prepare(k)
    for k in chain[last - 1]:
        hand(k)
    sw_begin()
    for level in range(last - 1, 0, -1):
        for k in near[level]:
            hand(k)
        for k in levels[level - 1]:
            prepare(k)
        for k in chain[level - 1]:
            hand(k)
        for k in chain[level] + near[level] if level == last - 1 else near[level] + chain[level]:
            settle(k)
    sw_planes()
    totals = settle(0)

    back = eye(rows)
    for a in range(2):
        turned = dot_nt(back, totals[a].astype(BF16)).astype(BF16)
        out4[:, :, a * pad : a * pad + feat] = turned.reshape(n_exp, slot, feat)
    for o in range(1, n_exp):
        swap(out4, in4, s4_sem, r4_sem, o).start()
    in4[pl.ds(e, 1)] = out4[pl.ds(e, 1)]
    sw_experts()

    remote(xq, xq, xq_s, xq_r, pair).wait_recv()
    remote(hq, hq, hq_s, hq_r, pair).wait_recv()

    @pl.loop(0, planes)
    def _(p):
        both = [xg[pl.ds(d * planes + p, 1)][0]] + [
            xq[o, pl.ds(p, 1)][0] for o in range(n_dp - 1)
        ]
        parts = [hid] + [hq.at[o] for o in range(n_dp - 1)]
        here = pl.ds(pl.multiple_of(p * Y * feat, Y * feat), Y * feat)
        for n, a, i in ((0, 0, 1), (1, 0, 2), (2, 1, 0)):
            total = None
            for b, h in zip(both, parts):
                term = dot(b[:, a].reshape(Y * feat, rows), h[:, i * hidw : (i + 1) * hidw])
                total = term if total is None else total + term
            grads_ref[n, here, :] = total.astype(BF16)

    stores = [
        pltpu.make_async_copy(src, dst, store_sem.at[i])
        for i, (src, dst) in enumerate(
            (
                (grads_ref.at[0], gate_grad_hbm),
                (grads_ref.at[1], up_grad_hbm),
                (grads_ref.at[2], down_grad_hbm),
                (mixed_ref, mixed_hbm),
                (in_grad_ref, in_grad_hbm),
                (logit_grad_ref, logit_grad_hbm),
            )
        )
    ]
    for store in stores[:3]:
        store.start()

    def sent(ref, sem):
        remote(ref, ref, sem, rg_sem.at[0], pair).wait_send()

    count, kept = len(others), nz - len(cross)
    sent(out0.at[pl.ds(0, n_exp - 1)], s0_sem)
    sent(xg.at[pl.ds(0, count), 0], sg_sem)
    sent(xg.at[pl.ds(0, nz - len(doubled)), 0], sy_sem)
    if doubled:
        sent(xg.at[pl.ds(0, len(doubled)), 0], sb_sem)
    sent(z_out.at[pl.ds(0, count)], sz_sem)
    sent(pair_out.at[pl.ds(0, kept)], sp_sem)
    sent(both_out, so_sem)
    sent(sw_z.at[pl.ds(0, nz - 1)], swz_s)
    sent(xq, xq_s)
    sent(hq, hq_s)
    sw_pair().wait_send()

    arrived = in4.at[pl.ds(0, n_exp - 1)]
    remote(arrived, arrived, s4_sem, r4_sem, pair).wait_recv()
    came = in4[...].reshape(rows, 2 * pad)
    picked = [dot(s, came) for s in select]
    mixed_ref[...] = (
        share[0] * picked[0][:, 0:feat] + share[1] * picked[1][:, 0:feat]
    ).astype(BF16)
    in_grad_ref[...] = (
        picked[0][:, pad : pad + feat] + picked[1][:, pad : pad + feat]
    ).astype(BF16)
    for store in stores[3:5]:
        store.start()
    arrived = sw_all.at[pl.ds(0, n_exp - 1)]
    remote(arrived, arrived, swx_s, swx_r, pair).wait_recv()
    sw = []
    for k in range(2):
        line = jnp.zeros((tok, rows), F32)
        for i in range(n_exp):
            line = line + hot[k][:, i : i + 1] * jnp.concatenate([sw_all[i]] * (tok // 8), axis=0)
        here = row_lane == e * slot + place[k]
        sw.append(jnp.sum(jnp.where(here, line, 0.0), axis=1, keepdims=True))
    first = jnp.sum(
        jnp.where(later == earlier, share[1] * sw[0] - share[0] * sw[1], 0.0),
        axis=0,
        keepdims=True,
    )
    which = lax.broadcasted_iota(jnp.int32, (2, tok), 0)
    logit_grad_ref[...] = jnp.where(which == 0, first, -first)
    stores[5].start()

    sent(out4.at[pl.ds(0, n_exp - 1)], s4_sem)
    sent(sw_all.at[pl.ds(0, n_exp - 1)], swx_s)
    for store in stores:
        store.wait()


def hand_over(*refs):
    count = (len(refs) - 2) // 3
    sources, results, held = refs[:count], refs[count : 2 * count], refs[2 * count : 3 * count]
    in_sem, out_sem = refs[-2:]
    ins = [pltpu.make_async_copy(sources[i], held[i], in_sem.at[i]) for i in range(count)]
    outs = [pltpu.make_async_copy(held[i], results[i], out_sem.at[i]) for i in range(count)]
    for copy in ins:
        copy.start()
    for before, after in zip(ins, outs):
        before.wait()
        after.start()
    for copy in outs:
        copy.wait()


def solution(mesh):
    n_dp, n_exp, n_t = mesh.shape["dp"], mesh.shape["expert"], mesh.shape["tensor"]
    nz = n_t // Y

    def on_device(tokens, expert_ids, gate_logits, gate_weight, up_weight, down_weight, out_grad):
        tok, feat = tokens.shape
        hidw = gate_weight.shape[2]
        slot = tok // 2
        rows = n_exp * slot
        planes = nz // n_dp
        pad = -(-feat // 128) * 128
        width = feat * n_t // n_dp
        hbm = pl.BlockSpec(memory_space=pl.ANY)
        dma = pltpu.SemaphoreType.DMA
        weights = [w.reshape(nz, Y * feat, hidw) for w in (gate_weight, up_weight, down_weight)]
        grad = jax.ShapeDtypeStruct((width, hidw), BF16)
        shapes = (
            jax.ShapeDtypeStruct((tok, feat), BF16),
            jax.ShapeDtypeStruct((tok, feat), BF16),
            jax.ShapeDtypeStruct((2, tok), F32),
            grad,
            grad,
            grad,
        )
        block = (2, feat, rows)
        outs = pl.pallas_call(
            functools.partial(kernel, (n_dp, n_exp, nz, tok, feat, hidw, pad)),
            out_shape=shapes,
            in_specs=[hbm] * 7,
            out_specs=[hbm] * 6,
            scratch_shapes=[
                pltpu.VMEM((tok, feat), BF16),
                pltpu.VMEM((2, tok), jnp.int32),
                pltpu.VMEM((2, tok), F32),
                pltpu.VMEM((tok, feat), BF16),
                pltpu.VMEM((tok, feat), BF16),
                pltpu.VMEM((tok, feat), BF16),
                pltpu.VMEM((2, tok), F32),
                pltpu.VMEM((3, width, hidw), BF16),
                pltpu.VMEM((nz, Y * feat, hidw), BF16),
                pltpu.VMEM((nz, Y * feat, hidw), BF16),
                pltpu.VMEM((nz, Y * feat, hidw), BF16),
                pltpu.VMEM((2 * tok, 2 * pad), BF16),
                pltpu.VMEM((n_exp, slot, 2 * pad), BF16),
                pltpu.VMEM((n_exp, slot, 2 * pad), BF16),
                pltpu.VMEM((nz, Y) + block, BF16),
                pltpu.VMEM((3, rows, hidw), F32),
                pltpu.VMEM((rows, 3 * hidw), BF16),
                pltpu.VMEM((n_dp - 1, planes, Y) + block, BF16),
                pltpu.VMEM((n_dp - 1, rows, 3 * hidw), BF16),
                pltpu.VMEM((nz, 2, Y, feat, rows), F32),
                pltpu.VMEM((nz,) + block, BF16),
                pltpu.VMEM((nz,) + block, BF16),
                pltpu.VMEM((nz,) + block, BF16),
                pltpu.VMEM((nz,) + block, BF16),
                pltpu.VMEM((3,) + block, BF16),
                pltpu.VMEM((3,) + block, BF16),
                pltpu.VMEM((nz, 8, rows), F32),
                pltpu.VMEM((Y, 8, rows), F32),
                pltpu.VMEM((n_exp, 8, rows), F32),
                pltpu.VMEM((n_exp, slot, 2 * pad), BF16),
                pltpu.VMEM((n_exp, slot, 2 * pad), BF16),
                dma((7,)),
                dma((6,)),
                dma,
                dma,
                dma,
                dma((nz,)),
                dma,
                dma((nz,)),
                dma,
                dma((3,)),
                dma,
                dma,
                dma,
                dma,
                dma,
                dma((nz,)),
                dma,
                dma((nz,)),
                dma,
                dma((3,)),
                dma,
                dma,
                dma,
                dma,
                dma,
                dma,
                dma,
                dma,
            ],
            compiler_params=pltpu.CompilerParams(
                collective_id=0, has_side_effects=True, vmem_limit_bytes=60 * 1024 * 1024
            ),
        )(tokens, expert_ids.T, gate_logits.T, *weights, out_grad)
        mixed, in_grad, logit_grad, gate_grad, up_grad, down_grad = pl.pallas_call(
            hand_over,
            out_shape=shapes,
            in_specs=[hbm] * 6,
            out_specs=[hbm] * 6,
            scratch_shapes=[pltpu.VMEM(out.shape, out.dtype) for out in shapes]
            + [dma((6,)), dma((6,))],
            compiler_params=pltpu.CompilerParams(vmem_limit_bytes=60 * 1024 * 1024),
        )(*outs)
        return mixed, in_grad, logit_grad.T, gate_grad[None], up_grad[None], down_grad[None]

    return jax.shard_map(
        on_device,
        mesh=mesh,
        in_specs=(
            P(("dp", "expert"), "tensor"),
            P(("dp", "expert"), None),
            P(("dp", "expert"), None),
            P("expert", None, "tensor"),
            P("expert", None, "tensor"),
            P("expert", None, "tensor"),
            P(("dp", "expert"), "tensor"),
        ),
        out_specs=(
            P(("dp", "expert"), "tensor"),
            P(("dp", "expert"), "tensor"),
            P(("dp", "expert"), None),
            P("expert", "dp", "tensor"),
            P("expert", "dp", "tensor"),
            P("expert", "dp", "tensor"),
        ),
        check_vma=False,
    )
```

```python
import functools

import jax
import jax.numpy as jnp
from jax import lax
from jax.experimental import pallas as pl
from jax.experimental.pallas import tpu as pltpu
from jax.sharding import PartitionSpec as P

MESH = pl.DeviceIdType.MESH
F32 = jnp.float32
BF16 = jnp.bfloat16
Y = 2


def dot(a, b):
    return jnp.dot(a, b, preferred_element_type=F32)


def dot_tn(a, b):
    return lax.dot_general(a, b, (((0,), (0,)), ((), ())), preferred_element_type=F32)


def dot_nt(a, b, precision=None):
    return lax.dot_general(
        a, b, (((1,), (1,)), ((), ())), precision=precision, preferred_element_type=F32
    )


def eye(n):
    rows = lax.broadcasted_iota(jnp.int32, (n, n), 0)
    cols = lax.broadcasted_iota(jnp.int32, (n, n), 1)
    return (rows == cols).astype(F32).astype(BF16)


def tree(nz):
    groups = nz // 4
    parent, levels = {}, [[0]]
    for i in range(groups):
        up, down = [2 * i + 2, 2 * i + 1], [-2 * i - 1]
        if i < groups - 1:
            down.insert(0, -2 * i - 2)
        parent.update({k: 2 * i for k in up})
        parent.update({k: -2 * i for k in down})
        levels.append([k for pair in zip(up, down) for k in pair] + up[len(down) :])
    end = 2 * groups
    doubled = [k for k in (3 - end, end - 1, 1 - end) if groups > 1 and parent[k] != 0]
    return parent, levels, doubled, {end: 2 - end, end - 1: end - 2, 1 - end: 2 - end}


def kernel(
    sizes,
    tok_hbm,
    ids_hbm,
    logit_hbm,
    wg_hbm,
    wu_hbm,
    wd_hbm,
    og_hbm,
    mixed_ref,
    in_grad_ref,
    logit_grad_ref,
    gate_grad_ref,
    up_grad_ref,
    down_grad_ref,
    tok_ref,
    ids_ref,
    logit_ref,
    og_ref,
    wg,
    wu,
    wd,
    stage,
    out0,
    in0,
    xg,
    acc,
    hid,
    xq,
    hq,
    terms,
    pair_out,
    pair_in,
    z_out,
    z_in,
    both_out,
    both_in,
    sw_z,
    sw_y,
    sw_all,
    out4,
    in4,
    load_sem,
    s0_sem,
    r0_sem,
    sy_sem,
    ry_sem,
    sg_sem,
    rg_sem,
    sb_sem,
    rb_sem,
    xq_s,
    xq_r,
    hq_s,
    hq_r,
    sp_sem,
    rp_sem,
    sz_sem,
    rz_sem,
    so_sem,
    ro_sem,
    swz_s,
    swz_r,
    swy_s,
    swy_r,
    swx_s,
    swx_r,
    s4_sem,
    r4_sem,
):
    n_dp, n_exp, nz, tok, feat, hidw, pad = sizes
    slot = tok // 2
    rows = n_exp * slot
    planes = nz // n_dp
    parent, levels, doubled, crossing = tree(nz)
    others = [k for level in levels[1:] for k in level]
    cross = list(crossing)
    children = {
        k: sorted((c for c in others if parent[c] == k), key=lambda c: -abs(c - k))
        for k in [0] + others
    }
    d = lax.axis_index("dp")
    e = lax.axis_index("expert")
    t_me = lax.axis_index("tensor")
    z, y = t_me // Y, t_me % Y
    y_other = 1 - y

    def at_z(off):
        return lax.rem(z + (off + nz), nz)

    def device(off, other=False):
        return {"tensor": at_z(off) * Y + (y_other if other else y)}

    def crossed(c):
        hop = c - crossing[c]
        return hop - nz if hop > 2 else hop

    pair = {"tensor": z * Y + y_other}

    hops = {k - parent[k] for k in others}
    z_peers = sorted({h % nz for h in hops} | {-h % nz for h in hops})
    peers = [device(off) for off in z_peers] + [pair]
    peers += [device(off, True) for off in z_peers]
    peers += [{"expert": lax.rem(e + o, n_exp)} for o in range(1, n_exp)]
    peers += [{"dp": lax.rem(d + o, n_dp)} for o in range(1, n_dp)]
    barrier = pltpu.get_barrier_semaphore()
    for peer in peers:
        pl.semaphore_signal(barrier, inc=1, device_id=peer, device_id_type=MESH)

    loads = [
        pltpu.make_async_copy(src, dst, load_sem.at[i])
        for i, (src, dst) in enumerate(
            (
                (ids_hbm, ids_ref),
                (logit_hbm, logit_ref),
                (tok_hbm, tok_ref),
                (og_hbm, og_ref),
                (wg_hbm, wg),
                (wu_hbm, wu),
                (wd_hbm, wd),
            )
        )
    ]
    for load in loads:
        load.start()

    def remote(src, dst, send, recv, peer):
        return pltpu.make_async_remote_copy(
            src_ref=src,
            dst_ref=dst,
            send_sem=send,
            recv_sem=recv,
            device_id=peer,
            device_id_type=MESH,
        )

    stage[...] = jnp.zeros_like(stage)
    out4[...] = jnp.zeros_like(out4)
    acc[...] = jnp.zeros_like(acc)
    later = lax.broadcasted_iota(jnp.int32, (tok, tok), 0)
    earlier = lax.broadcasted_iota(jnp.int32, (tok, tok), 1)
    before = (earlier < later).astype(F32).astype(BF16)
    lanes = lax.broadcasted_iota(jnp.int32, (tok, 128), 1)
    row_lane = lax.broadcasted_iota(jnp.int32, (tok, rows), 1)

    def column(line):
        return jnp.sum(jnp.where(later == earlier, line, 0), axis=1, keepdims=True)

    for load in loads[:2]:
        load.wait()
    ids = ids_ref[...].astype(F32)
    logits = logit_ref[...]
    id_k = [column(ids[k : k + 1, :]).astype(jnp.int32) for k in range(2)]
    hot = [(lanes == i).astype(F32) for i in id_k]
    count = dot(before, (hot[0] + hot[1]).astype(BF16))
    place = [jnp.sum(h * count, axis=1, keepdims=True).astype(jnp.int32) for h in hot]
    select = [
        (row_lane == i * slot + p).astype(F32).astype(BF16) for i, p in zip(id_k, place)
    ]
    diff = column(logits[0:1, :] - logits[1:2, :])
    share = (jax.nn.sigmoid(diff), jax.nn.sigmoid(-diff))

    for load in loads[2:4]:
        load.wait()
    tokens = tok_ref[...]
    grads = og_ref[...].astype(F32)
    for k in range(2):
        stage[k * tok : (k + 1) * tok, 0:feat] = tokens
        stage[k * tok : (k + 1) * tok, pad : pad + feat] = (share[k] * grads).astype(BF16)
    placed = dot_tn(jnp.concatenate(select, axis=0), stage[...]).astype(BF16)
    out0[...] = placed.reshape(n_exp, slot, 2 * pad)

    pl.semaphore_wait(barrier, len(peers))

    def swap(src, dst, send, recv, o):
        to = lax.rem(e + o, n_exp)
        return remote(src.at[to], dst.at[e], send, recv, {"expert": to})

    for o in range(1, n_exp):
        swap(out0, in0, s0_sem, r0_sem, o).start()
    in0[pl.ds(e, 1)] = out0[pl.ds(e, 1)]
    arrived = in0.at[pl.ds(0, n_exp - 1)]
    remote(arrived, arrived, s0_sem, r0_sem, pair).wait_recv()

    unit = eye(pad)
    for a in range(2):
        arrived = in0[:, :, a * pad : (a + 1) * pad].reshape(rows, pad)
        turned = dot_nt(unit, arrived)
        xg[pl.ds(z, 1), pl.ds(y, 1), a] = turned[0:feat].astype(BF16)[None, None]

    def deliver(c):
        ref = xg.at[at_z(-parent[c]), y]
        return remote(ref, ref, sg_sem, rg_sem.at[c % nz], device(c - parent[c]))

    def deliver_other(c):
        ref = xg.at[at_z(-parent[c]), y_other]
        n = doubled.index(c)
        return remote(ref, ref, sb_sem, rb_sem.at[n], device(c - parent[c]))

    def arrive(c):
        ref = xg.at[at_z(-c), y]
        remote(ref, ref, sg_sem, rg_sem.at[c % nz], device(c - parent[c])).wait_recv()

    def arrive_other(c):
        ref = xg.at[at_z(-c), y_other]
        n = doubled.index(c)
        remote(ref, ref, sb_sem, rb_sem.at[n], device(c - parent[c])).wait_recv()

    def across(k):
        ref = xg.at[at_z(-k), y]
        return remote(ref, ref, sy_sem, ry_sem.at[k % nz], pair)

    def complete(k):
        if k in doubled:
            arrive_other(k)
        else:
            across(k).wait_recv()
            for c in children[k]:
                if c in doubled:
                    deliver_other(c).start()

    def accumulate(block):
        both = xg[pl.ds(block, 1)]
        xt = both[0, :, 0].reshape(Y * feat, rows)
        gt = both[0, :, 1].reshape(Y * feat, rows)
        acc[0] += dot_tn(xt, wg[pl.ds(block, 1)][0])
        acc[1] += dot_tn(xt, wu[pl.ds(block, 1)][0])
        acc[2] += dot_tn(gt, wd[pl.ds(block, 1)][0])

    def forward(block):
        peer, p = block // planes, lax.rem(block, planes)
        o = lax.rem(peer - d + n_dp, n_dp)

        @pl.when(o > 0)
        def _():
            remote(
                xg.at[block],
                xq.at[o - 1, p],
                xq_s,
                xq_r,
                {"dp": peer},
            ).start()

    early = sorted({parent[c] for c in doubled})

    def use(level):
        for k in levels[level]:
            if k not in early:
                complete(k)
            accumulate(at_z(-k))
            forward(at_z(-k))

    last = len(levels) - 1
    for level, offsets in enumerate(levels):
        for k in offsets:
            if level > 0:
                arrive(k)
            for c in children[k]:
                if abs(c - k) > 1:
                    deliver(c).start()
            if k not in doubled:
                across(k).start()
            for c in children[k]:
                if abs(c - k) == 1:
                    deliver(c).start()
        if level == 0:
            for load in loads[4:]:
                load.wait()
        else:
            use(level - 1)
        for k in offsets:
            if k in early:
                complete(k)
    use(last)

    def factors(o):
        return remote(
            hid, hq.at[o - 1], hq_s, hq_r, {"dp": lax.rem(d + o, n_dp)}
        )

    gate, lift, hid_grad = acc[0], acc[1], acc[2]
    sigma = jax.nn.sigmoid(gate)
    active = gate * sigma
    hidden = active * lift
    hid[:, 0:hidw] = hidden.astype(BF16)
    hid[:, hidw : 2 * hidw] = (
        hid_grad * lift * sigma * (1.0 + gate * (1.0 - sigma))
    ).astype(BF16)
    hid[:, 2 * hidw : 3 * hidw] = (hid_grad * active).astype(BF16)

    def own(block, a):
        if a == 0:
            return dot_nt(wd[pl.ds(block, 1)][0], hid[:, 0:hidw])
        return dot_nt(wg[pl.ds(block, 1)][0], hid[:, hidw : 2 * hidw]) + dot_nt(
            wu[pl.ds(block, 1)][0], hid[:, 2 * hidw : 3 * hidw]
        )

    def to_pair(k):
        n = k % nz
        return remote(pair_out.at[n], pair_in.at[n], sp_sem, rp_sem.at[n], pair)

    def along(k):
        n = k % nz
        return remote(
            z_out.at[n], z_in.at[n], sz_sem, rz_sem.at[n], device(parent[k] - k)
        )

    def along_across(k):
        n = cross.index(k)
        return remote(
            both_out.at[n], both_in.at[n], so_sem, ro_sem.at[n], device(-crossed(k), True)
        )

    def prepare(k):
        n = k % nz
        for a in range(2):
            terms[n, a] = own(at_z(-k), a).reshape(Y, feat, rows)
            if k in crossing:
                z_out[n, a] = terms[n, a, pl.ds(y, 1)][0].astype(BF16)
                both_out[cross.index(k), a] = terms[n, a, pl.ds(y_other, 1)][0].astype(BF16)
        if k in crossing:
            along(k).start()
            along_across(k).start()

    def hand(k):
        n = k % nz
        for a in range(2):
            pair_out[n, a] = terms[n, a, pl.ds(y_other, 1)][0].astype(BF16)
        to_pair(k).start()

    def settle(k):
        n = k % nz
        to_pair(k).wait_recv()
        for c in children[k]:
            along(c).wait_recv()
        over = [c for c in cross if crossing[c] == k]
        for c in over:
            along_across(c).wait_recv()
        totals = []
        for a in range(2):
            total = terms[n, a, pl.ds(y, 1)][0] + pair_in[n, a].astype(F32)
            for c in children[k]:
                total = total + z_in[c % nz, a].astype(F32)
            for c in over:
                total = total + both_in[cross.index(c), a].astype(F32)
            if k != 0:
                z_out[n, a] = total.astype(BF16)
            totals.append(total)
        if k != 0:
            along(k).start()
        return totals

    chain = [[k for k in level if children[k]] for level in levels]
    near = [[k for k in level if not children[k]] for level in levels]
    for k in levels[last]:
        prepare(k)
    for o in range(1, n_dp):
        factors(o).start()

    def sw_send(off):
        ref = sw_z.at[z]
        return remote(ref, ref, swz_s, swz_r, device(off))

    def sw_pair():
        return remote(sw_y.at[y], sw_y.at[y], swy_s, swy_r, pair)

    def sw_swap(o):
        return remote(
            sw_all.at[e],
            sw_all.at[e],
            swx_s,
            swx_r,
            {"expert": lax.rem(e + o, n_exp)},
        )

    line = dot_nt(jnp.ones((8, hidw), F32), hidden * hid_grad, lax.Precision.HIGHEST)
    sw_z[pl.ds(z, 1)] = line[None]

    def sw_begin():
        for off in range(1, nz):
            sw_send(off).start()

    def sw_planes():
        arrived = sw_z.at[pl.ds(0, nz - 1)]
        remote(arrived, arrived, swz_s, swz_r, pair).wait_recv()
        total = sw_z[0]
        for i in range(1, nz):
            total = total + sw_z[i]
        sw_y[pl.ds(y, 1)] = total[None]
        sw_pair().start()

    def sw_experts():
        sw_pair().wait_recv()
        sw_all[pl.ds(e, 1)] = (sw_y[0] + sw_y[1])[None]
        for o in range(1, n_exp):
            sw_swap(o).start()

    for k in levels[last - 1]:
        prepare(k)
    for k in chain[last - 1]:
        hand(k)
    sw_begin()
    for level in range(last - 1, 0, -1):
        for k in near[level]:
            hand(k)
        for k in levels[level - 1]:
            prepare(k)
        for k in chain[level - 1]:
            hand(k)
        for k in chain[level] + near[level] if level == last - 1 else near[level] + chain[level]:
            settle(k)
    sw_planes()
    totals = settle(0)

    back = eye(rows)
    for a in range(2):
        turned = dot_nt(back, totals[a].astype(BF16)).astype(BF16)
        out4[:, :, a * pad : a * pad + feat] = turned.reshape(n_exp, slot, feat)
    for o in range(1, n_exp):
        swap(out4, in4, s4_sem, r4_sem, o).start()
    in4[pl.ds(e, 1)] = out4[pl.ds(e, 1)]
    sw_experts()

    remote(xq, xq, xq_s, xq_r, pair).wait_recv()
    remote(hq, hq, hq_s, hq_r, pair).wait_recv()

    @pl.loop(0, planes)
    def _(p):
        both = [xg[pl.ds(d * planes + p, 1)][0]] + [
            xq[o, pl.ds(p, 1)][0] for o in range(n_dp - 1)
        ]
        parts = [hid] + [hq.at[o] for o in range(n_dp - 1)]
        here = pl.ds(pl.multiple_of(p * Y * feat, Y * feat), Y * feat)
        for ref, a, i in ((gate_grad_ref, 0, 1), (up_grad_ref, 0, 2), (down_grad_ref, 1, 0)):
            total = None
            for b, h in zip(both, parts):
                term = dot(b[:, a].reshape(Y * feat, rows), h[:, i * hidw : (i + 1) * hidw])
                total = term if total is None else total + term
            ref[here, :] = total.astype(BF16)

    def sent(ref, sem):
        remote(ref, ref, sem, rg_sem.at[0], pair).wait_send()

    count, kept = len(others), nz - len(cross)
    sent(out0.at[pl.ds(0, n_exp - 1)], s0_sem)
    sent(xg.at[pl.ds(0, count), 0], sg_sem)
    sent(xg.at[pl.ds(0, nz - len(doubled)), 0], sy_sem)
    if doubled:
        sent(xg.at[pl.ds(0, len(doubled)), 0], sb_sem)
    sent(z_out.at[pl.ds(0, count)], sz_sem)
    sent(pair_out.at[pl.ds(0, kept)], sp_sem)
    sent(both_out, so_sem)
    sent(sw_z.at[pl.ds(0, nz - 1)], swz_s)
    sent(xq, xq_s)
    sent(hq, hq_s)
    sw_pair().wait_send()

    arrived = in4.at[pl.ds(0, n_exp - 1)]
    remote(arrived, arrived, s4_sem, r4_sem, pair).wait_recv()
    came = in4[...].reshape(rows, 2 * pad)
    picked = [dot(s, came) for s in select]
    mixed_ref[...] = (
        share[0] * picked[0][:, 0:feat] + share[1] * picked[1][:, 0:feat]
    ).astype(BF16)
    in_grad_ref[...] = (
        picked[0][:, pad : pad + feat] + picked[1][:, pad : pad + feat]
    ).astype(BF16)
    arrived = sw_all.at[pl.ds(0, n_exp - 1)]
    remote(arrived, arrived, swx_s, swx_r, pair).wait_recv()
    sw = []
    for k in range(2):
        line = jnp.zeros((tok, rows), F32)
        for i in range(n_exp):
            line = line + hot[k][:, i : i + 1] * jnp.concatenate([sw_all[i]] * (tok // 8), axis=0)
        here = row_lane == e * slot + place[k]
        sw.append(jnp.sum(jnp.where(here, line, 0.0), axis=1, keepdims=True))
    first = jnp.sum(
        jnp.where(later == earlier, share[1] * sw[0] - share[0] * sw[1], 0.0),
        axis=0,
        keepdims=True,
    )
    which = lax.broadcasted_iota(jnp.int32, (2, tok), 0)
    logit_grad_ref[...] = jnp.where(which == 0, first, -first)

    sent(out4.at[pl.ds(0, n_exp - 1)], s4_sem)
    sent(sw_all.at[pl.ds(0, n_exp - 1)], swx_s)


def hand_over(*refs):
    count = len(refs) // 2
    sem = refs[-1]
    copies = [
        pltpu.make_async_copy(refs[i], refs[count + i], sem.at[i]) for i in range(count)
    ]
    for copy in copies:
        copy.start()
    for copy in copies:
        copy.wait()


def solution(mesh):
    n_dp, n_exp, n_t = mesh.shape["dp"], mesh.shape["expert"], mesh.shape["tensor"]
    nz = n_t // Y

    def on_device(tokens, expert_ids, gate_logits, gate_weight, up_weight, down_weight, out_grad):
        tok, feat = tokens.shape
        hidw = gate_weight.shape[2]
        slot = tok // 2
        rows = n_exp * slot
        planes = nz // n_dp
        pad = -(-feat // 128) * 128
        width = feat * n_t // n_dp
        hbm = pl.BlockSpec(memory_space=pl.ANY)
        vmem = pl.BlockSpec(memory_space=pltpu.VMEM)
        dma = pltpu.SemaphoreType.DMA
        weights = [w.reshape(nz, Y * feat, hidw) for w in (gate_weight, up_weight, down_weight)]
        grad = jax.ShapeDtypeStruct((width, hidw), BF16)
        shapes = (
            jax.ShapeDtypeStruct((tok, feat), BF16),
            jax.ShapeDtypeStruct((tok, feat), BF16),
            jax.ShapeDtypeStruct((2, tok), F32),
            grad,
            grad,
            grad,
        )
        block = (2, feat, rows)
        outs = pl.pallas_call(
            functools.partial(kernel, (n_dp, n_exp, nz, tok, feat, hidw, pad)),
            out_shape=tuple(pltpu.VMEM(out.shape, out.dtype) for out in shapes),
            in_specs=[hbm] * 7,
            out_specs=[vmem] * 6,
            scratch_shapes=[
                pltpu.VMEM((tok, feat), BF16),
                pltpu.VMEM((2, tok), jnp.int32),
                pltpu.VMEM((2, tok), F32),
                pltpu.VMEM((tok, feat), BF16),
                pltpu.VMEM((nz, Y * feat, hidw), BF16),
                pltpu.VMEM((nz, Y * feat, hidw), BF16),
                pltpu.VMEM((nz, Y * feat, hidw), BF16),
                pltpu.VMEM((2 * tok, 2 * pad), BF16),
                pltpu.VMEM((n_exp, slot, 2 * pad), BF16),
                pltpu.VMEM((n_exp, slot, 2 * pad), BF16),
                pltpu.VMEM((nz, Y) + block, BF16),
                pltpu.VMEM((3, rows, hidw), F32),
                pltpu.VMEM((rows, 3 * hidw), BF16),
                pltpu.VMEM((n_dp - 1, planes, Y) + block, BF16),
                pltpu.VMEM((n_dp - 1, rows, 3 * hidw), BF16),
                pltpu.VMEM((nz, 2, Y, feat, rows), F32),
                pltpu.VMEM((nz,) + block, BF16),
                pltpu.VMEM((nz,) + block, BF16),
                pltpu.VMEM((nz,) + block, BF16),
                pltpu.VMEM((nz,) + block, BF16),
                pltpu.VMEM((3,) + block, BF16),
                pltpu.VMEM((3,) + block, BF16),
                pltpu.VMEM((nz, 8, rows), F32),
                pltpu.VMEM((Y, 8, rows), F32),
                pltpu.VMEM((n_exp, 8, rows), F32),
                pltpu.VMEM((n_exp, slot, 2 * pad), BF16),
                pltpu.VMEM((n_exp, slot, 2 * pad), BF16),
                dma((7,)),
                dma,
                dma,
                dma,
                dma((nz,)),
                dma,
                dma((nz,)),
                dma,
                dma((3,)),
                dma,
                dma,
                dma,
                dma,
                dma,
                dma((nz,)),
                dma,
                dma((nz,)),
                dma,
                dma((3,)),
                dma,
                dma,
                dma,
                dma,
                dma,
                dma,
                dma,
                dma,
            ],
            compiler_params=pltpu.CompilerParams(
                collective_id=0, has_side_effects=True, vmem_limit_bytes=60 * 1024 * 1024
            ),
        )(tokens, expert_ids.T, gate_logits.T, *weights, out_grad)
        mixed, in_grad, logit_grad, gate_grad, up_grad, down_grad = pl.pallas_call(
            hand_over,
            out_shape=shapes,
            in_specs=[vmem] * 6,
            out_specs=[hbm] * 6,
            scratch_shapes=[dma((6,))],
            compiler_params=pltpu.CompilerParams(vmem_limit_bytes=4 * 1024 * 1024),
        )(*outs)
        return mixed, in_grad, logit_grad.T, gate_grad[None], up_grad[None], down_grad[None]

    return jax.shard_map(
        on_device,
        mesh=mesh,
        in_specs=(
            P(("dp", "expert"), "tensor"),
            P(("dp", "expert"), None),
            P(("dp", "expert"), None),
            P("expert", None, "tensor"),
            P("expert", None, "tensor"),
            P("expert", None, "tensor"),
            P(("dp", "expert"), "tensor"),
        ),
        out_specs=(
            P(("dp", "expert"), "tensor"),
            P(("dp", "expert"), "tensor"),
            P(("dp", "expert"), None),
            P("expert", "dp", "tensor"),
            P("expert", "dp", "tensor"),
            P("expert", "dp", "tensor"),
        ),
        check_vma=False,
    )
```

```python
import functools

import jax
import jax.numpy as jnp
from jax import lax
from jax.experimental import pallas as pl
from jax.experimental.pallas import tpu as pltpu
from jax.sharding import PartitionSpec as P

MESH = pl.DeviceIdType.MESH
F32 = jnp.float32
BF16 = jnp.bfloat16
Y = 2


def dot(a, b):
    return jnp.dot(a, b, preferred_element_type=F32)


def dot_tn(a, b):
    return lax.dot_general(a, b, (((0,), (0,)), ((), ())), preferred_element_type=F32)


def dot_nt(a, b, precision=None):
    return lax.dot_general(
        a, b, (((1,), (1,)), ((), ())), precision=precision, preferred_element_type=F32
    )


def eye(n):
    rows = lax.broadcasted_iota(jnp.int32, (n, n), 0)
    cols = lax.broadcasted_iota(jnp.int32, (n, n), 1)
    return (rows == cols).astype(F32).astype(BF16)


def tree(nz):
    groups = nz // 4
    parent, levels = {}, [[0]]
    for i in range(groups):
        up, down = [2 * i + 2, 2 * i + 1], [-2 * i - 1]
        if i < groups - 1:
            down.insert(0, -2 * i - 2)
        parent.update({k: 2 * i for k in up})
        parent.update({k: -2 * i for k in down})
        levels.append([k for pair in zip(up, down) for k in pair] + up[len(down) :])
    end = 2 * groups
    doubled = [k for k in (3 - end, end - 1, 1 - end) if groups > 1 and parent[k] != 0]
    return parent, levels, doubled


def kernel(
    sizes,
    tok_hbm,
    ids_hbm,
    logit_hbm,
    wg_hbm,
    wu_hbm,
    wd_hbm,
    og_hbm,
    mixed_ref,
    in_grad_ref,
    logit_grad_ref,
    gate_grad_ref,
    up_grad_ref,
    down_grad_ref,
    tok_ref,
    ids_ref,
    logit_ref,
    og_ref,
    wg,
    wu,
    wd,
    stage,
    out0,
    in0,
    xg,
    acc,
    hid,
    xq,
    hq,
    terms,
    pair_out,
    pair_in,
    z_out,
    z_in,
    sw_z,
    sw_y,
    sw_all,
    out4,
    in4,
    load_sem,
    s0_sem,
    r0_sem,
    sy_sem,
    ry_sem,
    sg_sem,
    rg_sem,
    sb_sem,
    rb_sem,
    xq_s,
    xq_r,
    hq_s,
    hq_r,
    sp_sem,
    rp_sem,
    sz_sem,
    rz_sem,
    swz_s,
    swz_r,
    swy_s,
    swy_r,
    swx_s,
    swx_r,
    s4_sem,
    r4_sem,
):
    n_dp, n_exp, nz, tok, feat, hidw, pad = sizes
    slot = tok // 2
    rows = n_exp * slot
    planes = nz // n_dp
    parent, levels, doubled = tree(nz)
    others = [k for level in levels[1:] for k in level]
    children = {
        k: sorted((c for c in others if parent[c] == k), key=lambda c: -abs(c - k))
        for k in [0] + others
    }
    d = lax.axis_index("dp")
    e = lax.axis_index("expert")
    t_me = lax.axis_index("tensor")
    z, y = t_me // Y, t_me % Y
    y_other = 1 - y

    def at_z(off):
        return lax.rem(z + (off + nz), nz)

    def device(off):
        return {"tensor": at_z(off) * Y + y}

    pair = {"tensor": z * Y + y_other}

    hops = {k - parent[k] for k in others}
    z_peers = sorted({h % nz for h in hops} | {-h % nz for h in hops})
    peers = [device(off) for off in z_peers] + [pair]
    peers += [{"expert": lax.rem(e + o, n_exp)} for o in range(1, n_exp)]
    peers += [{"dp": lax.rem(d + o, n_dp)} for o in range(1, n_dp)]
    barrier = pltpu.get_barrier_semaphore()
    for peer in peers:
        pl.semaphore_signal(barrier, inc=1, device_id=peer, device_id_type=MESH)

    loads = [
        pltpu.make_async_copy(src, dst, load_sem.at[i])
        for i, (src, dst) in enumerate(
            (
                (ids_hbm, ids_ref),
                (logit_hbm, logit_ref),
                (tok_hbm, tok_ref),
                (og_hbm, og_ref),
                (wg_hbm, wg),
                (wu_hbm, wu),
                (wd_hbm, wd),
            )
        )
    ]
    for load in loads:
        load.start()

    def remote(src, dst, send, recv, peer):
        return pltpu.make_async_remote_copy(
            src_ref=src,
            dst_ref=dst,
            send_sem=send,
            recv_sem=recv,
            device_id=peer,
            device_id_type=MESH,
        )

    stage[...] = jnp.zeros_like(stage)
    out4[...] = jnp.zeros_like(out4)
    acc[...] = jnp.zeros_like(acc)
    later = lax.broadcasted_iota(jnp.int32, (tok, tok), 0)
    earlier = lax.broadcasted_iota(jnp.int32, (tok, tok), 1)
    before = (earlier < later).astype(F32).astype(BF16)
    lanes = lax.broadcasted_iota(jnp.int32, (tok, 128), 1)
    row_lane = lax.broadcasted_iota(jnp.int32, (tok, rows), 1)

    def column(line):
        return jnp.sum(jnp.where(later == earlier, line, 0), axis=1, keepdims=True)

    for load in loads[:2]:
        load.wait()
    ids = ids_ref[...].astype(F32)
    logits = logit_ref[...]
    id_k = [column(ids[k : k + 1, :]).astype(jnp.int32) for k in range(2)]
    hot = [(lanes == i).astype(F32) for i in id_k]
    count = dot(before, (hot[0] + hot[1]).astype(BF16))
    place = [jnp.sum(h * count, axis=1, keepdims=True).astype(jnp.int32) for h in hot]
    select = [
        (row_lane == i * slot + p).astype(F32).astype(BF16) for i, p in zip(id_k, place)
    ]
    diff = column(logits[0:1, :] - logits[1:2, :])
    share = (jax.nn.sigmoid(diff), jax.nn.sigmoid(-diff))

    for load in loads[2:4]:
        load.wait()
    tokens = tok_ref[...]
    grads = og_ref[...].astype(F32)
    for k in range(2):
        stage[k * tok : (k + 1) * tok, 0:feat] = tokens
        stage[k * tok : (k + 1) * tok, pad : pad + feat] = (share[k] * grads).astype(BF16)
    placed = dot_tn(jnp.concatenate(select, axis=0), stage[...]).astype(BF16)
    out0[...] = placed.reshape(n_exp, slot, 2 * pad)

    pl.semaphore_wait(barrier, len(peers))

    def swap(src, dst, send, recv, o):
        to = lax.rem(e + o, n_exp)
        return remote(src.at[to], dst.at[e], send, recv, {"expert": to})

    for o in range(1, n_exp):
        swap(out0, in0, s0_sem, r0_sem, o).start()
    in0[pl.ds(e, 1)] = out0[pl.ds(e, 1)]
    arrived = in0.at[pl.ds(0, n_exp - 1)]
    remote(arrived, arrived, s0_sem, r0_sem, pair).wait_recv()

    unit = eye(pad)
    for a in range(2):
        arrived = in0[:, :, a * pad : (a + 1) * pad].reshape(rows, pad)
        turned = dot_nt(unit, arrived)
        xg[pl.ds(z, 1), pl.ds(y, 1), a] = turned[0:feat].astype(BF16)[None, None]

    def deliver(c):
        ref = xg.at[at_z(-parent[c]), y]
        return remote(ref, ref, sg_sem, rg_sem.at[c % nz], device(c - parent[c]))

    def deliver_other(c):
        ref = xg.at[at_z(-parent[c]), y_other]
        n = doubled.index(c)
        return remote(ref, ref, sb_sem, rb_sem.at[n], device(c - parent[c]))

    def arrive(c):
        ref = xg.at[at_z(-c), y]
        remote(ref, ref, sg_sem, rg_sem.at[c % nz], device(c - parent[c])).wait_recv()

    def arrive_other(c):
        ref = xg.at[at_z(-c), y_other]
        n = doubled.index(c)
        remote(ref, ref, sb_sem, rb_sem.at[n], device(c - parent[c])).wait_recv()

    def across(k):
        ref = xg.at[at_z(-k), y]
        return remote(ref, ref, sy_sem, ry_sem.at[k % nz], pair)

    def complete(k):
        if k in doubled:
            arrive_other(k)
        else:
            across(k).wait_recv()
            for c in children[k]:
                if c in doubled:
                    deliver_other(c).start()

    def accumulate(block):
        both = xg[pl.ds(block, 1)]
        xt = both[0, :, 0].reshape(Y * feat, rows)
        gt = both[0, :, 1].reshape(Y * feat, rows)
        acc[0] += dot_tn(xt, wg[pl.ds(block, 1)][0])
        acc[1] += dot_tn(xt, wu[pl.ds(block, 1)][0])
        acc[2] += dot_tn(gt, wd[pl.ds(block, 1)][0])

    def forward(block):
        peer, p = block // planes, lax.rem(block, planes)
        o = lax.rem(peer - d + n_dp, n_dp)

        @pl.when(o > 0)
        def _():
            remote(
                xg.at[block],
                xq.at[o - 1, p],
                xq_s,
                xq_r,
                {"dp": peer},
            ).start()

    early = sorted({parent[c] for c in doubled})

    def use(level):
        for k in levels[level]:
            if k not in early:
                complete(k)
            accumulate(at_z(-k))
            forward(at_z(-k))

    last = len(levels) - 1
    for level, offsets in enumerate(levels):
        for k in offsets:
            if level > 0:
                arrive(k)
            for c in children[k]:
                if abs(c - k) > 1:
                    deliver(c).start()
            if k not in doubled:
                across(k).start()
            for c in children[k]:
                if abs(c - k) == 1:
                    deliver(c).start()
        if level == 0:
            for load in loads[4:]:
                load.wait()
        else:
            use(level - 1)
        for k in offsets:
            if k in early:
                complete(k)
    use(last)

    def factors(o):
        return remote(
            hid, hq.at[o - 1], hq_s, hq_r, {"dp": lax.rem(d + o, n_dp)}
        )

    gate, lift, hid_grad = acc[0], acc[1], acc[2]
    sigma = jax.nn.sigmoid(gate)
    active = gate * sigma
    hidden = active * lift
    hid[:, 0:hidw] = hidden.astype(BF16)
    hid[:, hidw : 2 * hidw] = (
        hid_grad * lift * sigma * (1.0 + gate * (1.0 - sigma))
    ).astype(BF16)
    hid[:, 2 * hidw : 3 * hidw] = (hid_grad * active).astype(BF16)

    def own(block, a):
        if a == 0:
            return dot_nt(wd[pl.ds(block, 1)][0], hid[:, 0:hidw])
        return dot_nt(wg[pl.ds(block, 1)][0], hid[:, hidw : 2 * hidw]) + dot_nt(
            wu[pl.ds(block, 1)][0], hid[:, 2 * hidw : 3 * hidw]
        )

    def to_pair(k):
        n = k % nz
        return remote(pair_out.at[n], pair_in.at[n], sp_sem, rp_sem.at[n], pair)

    def along(k):
        n = k % nz
        return remote(
            z_out.at[n], z_in.at[n], sz_sem, rz_sem.at[n], device(parent[k] - k)
        )

    def prepare(k):
        n = k % nz
        for a in range(2):
            terms[n, a] = own(at_z(-k), a).reshape(Y, feat, rows)
    def hand(k):
        n = k % nz
        for a in range(2):
            pair_out[n, a] = terms[n, a, pl.ds(y_other, 1)][0].astype(BF16)
        to_pair(k).start()

    def settle(k):
        n = k % nz
        to_pair(k).wait_recv()
        for c in children[k]:
            along(c).wait_recv()
        totals = []
        for a in range(2):
            total = terms[n, a, pl.ds(y, 1)][0] + pair_in[n, a].astype(F32)
            for c in children[k]:
                total = total + z_in[c % nz, a].astype(F32)
            if k != 0:
                z_out[n, a] = total.astype(BF16)
            totals.append(total)
        if k != 0:
            along(k).start()
        return totals

    chain = [[k for k in level if children[k]] for level in levels]
    near = [[k for k in level if not children[k]] for level in levels]
    for k in levels[last]:
        prepare(k)
        hand(k)
    for o in range(1, n_dp):
        factors(o).start()

    def sw_send(off):
        ref = sw_z.at[z]
        return remote(ref, ref, swz_s, swz_r, device(off))

    def sw_pair():
        return remote(sw_y.at[y], sw_y.at[y], swy_s, swy_r, pair)

    def sw_swap(o):
        return remote(
            sw_all.at[e],
            sw_all.at[e],
            swx_s,
            swx_r,
            {"expert": lax.rem(e + o, n_exp)},
        )

    line = dot_nt(jnp.ones((8, hidw), F32), hidden * hid_grad, lax.Precision.HIGHEST)
    sw_z[pl.ds(z, 1)] = line[None]

    def sw_begin():
        for off in range(1, nz):
            sw_send(off).start()

    def sw_planes():
        arrived = sw_z.at[pl.ds(0, nz - 1)]
        remote(arrived, arrived, swz_s, swz_r, pair).wait_recv()
        total = sw_z[0]
        for i in range(1, nz):
            total = total + sw_z[i]
        sw_y[pl.ds(y, 1)] = total[None]
        sw_pair().start()

    def sw_experts():
        sw_pair().wait_recv()
        sw_all[pl.ds(e, 1)] = (sw_y[0] + sw_y[1])[None]
        for o in range(1, n_exp):
            sw_swap(o).start()

    for k in levels[last - 1]:
        prepare(k)
    for k in chain[last - 1]:
        hand(k)
    for k in levels[last]:
        settle(k)
    sw_begin()
    for k in near[last - 1]:
        hand(k)
    for level in range(last - 1, 0, -1):
        for k in levels[level - 1]:
            prepare(k)
        for k in chain[level - 1] + near[level - 1]:
            hand(k)
        for k in near[level] + chain[level]:
            settle(k)
    sw_planes()
    totals = settle(0)

    back = eye(rows)
    for a in range(2):
        turned = dot_nt(back, totals[a].astype(BF16)).astype(BF16)
        out4[:, :, a * pad : a * pad + feat] = turned.reshape(n_exp, slot, feat)
    for o in range(1, n_exp):
        swap(out4, in4, s4_sem, r4_sem, o).start()
    in4[pl.ds(e, 1)] = out4[pl.ds(e, 1)]
    sw_experts()

    remote(xq, xq, xq_s, xq_r, pair).wait_recv()
    remote(hq, hq, hq_s, hq_r, pair).wait_recv()

    @pl.loop(0, planes)
    def _(p):
        both = [xg[pl.ds(d * planes + p, 1)][0]] + [
            xq[o, pl.ds(p, 1)][0] for o in range(n_dp - 1)
        ]
        parts = [hid] + [hq.at[o] for o in range(n_dp - 1)]
        here = pl.ds(pl.multiple_of(p * Y * feat, Y * feat), Y * feat)
        for ref, a, i in ((gate_grad_ref, 0, 1), (up_grad_ref, 0, 2), (down_grad_ref, 1, 0)):
            total = None
            for b, h in zip(both, parts):
                term = dot(b[:, a].reshape(Y * feat, rows), h[:, i * hidw : (i + 1) * hidw])
                total = term if total is None else total + term
            ref[here, :] = total.astype(BF16)

    def sent(ref, sem):
        remote(ref, ref, sem, rg_sem.at[0], pair).wait_send()

    count = len(others)
    sent(out0.at[pl.ds(0, n_exp - 1)], s0_sem)
    sent(xg.at[pl.ds(0, count), 0], sg_sem)
    sent(xg.at[pl.ds(0, nz - len(doubled)), 0], sy_sem)
    if doubled:
        sent(xg.at[pl.ds(0, len(doubled)), 0], sb_sem)
    sent(z_out.at[pl.ds(0, count)], sz_sem)
    sent(pair_out, sp_sem)
    sent(sw_z.at[pl.ds(0, nz - 1)], swz_s)
    sent(xq, xq_s)
    sent(hq, hq_s)
    sw_pair().wait_send()

    arrived = in4.at[pl.ds(0, n_exp - 1)]
    remote(arrived, arrived, s4_sem, r4_sem, pair).wait_recv()
    came = in4[...].reshape(rows, 2 * pad)
    picked = [dot(s, came) for s in select]
    mixed_ref[...] = (
        share[0] * picked[0][:, 0:feat] + share[1] * picked[1][:, 0:feat]
    ).astype(BF16)
    in_grad_ref[...] = (
        picked[0][:, pad : pad + feat] + picked[1][:, pad : pad + feat]
    ).astype(BF16)
    arrived = sw_all.at[pl.ds(0, n_exp - 1)]
    remote(arrived, arrived, swx_s, swx_r, pair).wait_recv()
    sw = []
    for k in range(2):
        line = jnp.zeros((tok, rows), F32)
        for i in range(n_exp):
            line = line + hot[k][:, i : i + 1] * jnp.concatenate([sw_all[i]] * (tok // 8), axis=0)
        here = row_lane == e * slot + place[k]
        sw.append(jnp.sum(jnp.where(here, line, 0.0), axis=1, keepdims=True))
    first = jnp.sum(
        jnp.where(later == earlier, share[1] * sw[0] - share[0] * sw[1], 0.0),
        axis=0,
        keepdims=True,
    )
    which = lax.broadcasted_iota(jnp.int32, (2, tok), 0)
    logit_grad_ref[...] = jnp.where(which == 0, first, -first)

    sent(out4.at[pl.ds(0, n_exp - 1)], s4_sem)
    sent(sw_all.at[pl.ds(0, n_exp - 1)], swx_s)


def hand_over(*refs):
    count = len(refs) // 2
    sem = refs[-1]
    copies = [
        pltpu.make_async_copy(refs[i], refs[count + i], sem.at[i]) for i in range(count)
    ]
    for copy in copies:
        copy.start()
    for copy in copies:
        copy.wait()


def solution(mesh):
    n_dp, n_exp, n_t = mesh.shape["dp"], mesh.shape["expert"], mesh.shape["tensor"]
    nz = n_t // Y

    def on_device(tokens, expert_ids, gate_logits, gate_weight, up_weight, down_weight, out_grad):
        tok, feat = tokens.shape
        hidw = gate_weight.shape[2]
        slot = tok // 2
        rows = n_exp * slot
        planes = nz // n_dp
        pad = -(-feat // 128) * 128
        width = feat * n_t // n_dp
        hbm = pl.BlockSpec(memory_space=pl.ANY)
        vmem = pl.BlockSpec(memory_space=pltpu.VMEM)
        dma = pltpu.SemaphoreType.DMA
        weights = [w.reshape(nz, Y * feat, hidw) for w in (gate_weight, up_weight, down_weight)]
        grad = jax.ShapeDtypeStruct((width, hidw), BF16)
        shapes = (
            jax.ShapeDtypeStruct((tok, feat), BF16),
            jax.ShapeDtypeStruct((tok, feat), BF16),
            jax.ShapeDtypeStruct((2, tok), F32),
            grad,
            grad,
            grad,
        )
        block = (2, feat, rows)
        outs = pl.pallas_call(
            functools.partial(kernel, (n_dp, n_exp, nz, tok, feat, hidw, pad)),
            out_shape=tuple(pltpu.VMEM(out.shape, out.dtype) for out in shapes),
            in_specs=[hbm] * 7,
            out_specs=[vmem] * 6,
            scratch_shapes=[
                pltpu.VMEM((tok, feat), BF16),
                pltpu.VMEM((2, tok), jnp.int32),
                pltpu.VMEM((2, tok), F32),
                pltpu.VMEM((tok, feat), BF16),
                pltpu.VMEM((nz, Y * feat, hidw), BF16),
                pltpu.VMEM((nz, Y * feat, hidw), BF16),
                pltpu.VMEM((nz, Y * feat, hidw), BF16),
                pltpu.VMEM((2 * tok, 2 * pad), BF16),
                pltpu.VMEM((n_exp, slot, 2 * pad), BF16),
                pltpu.VMEM((n_exp, slot, 2 * pad), BF16),
                pltpu.VMEM((nz, Y) + block, BF16),
                pltpu.VMEM((3, rows, hidw), F32),
                pltpu.VMEM((rows, 3 * hidw), BF16),
                pltpu.VMEM((n_dp - 1, planes, Y) + block, BF16),
                pltpu.VMEM((n_dp - 1, rows, 3 * hidw), BF16),
                pltpu.VMEM((nz, 2, Y, feat, rows), F32),
                pltpu.VMEM((nz,) + block, BF16),
                pltpu.VMEM((nz,) + block, BF16),
                pltpu.VMEM((nz,) + block, BF16),
                pltpu.VMEM((nz,) + block, BF16),
                pltpu.VMEM((nz, 8, rows), F32),
                pltpu.VMEM((Y, 8, rows), F32),
                pltpu.VMEM((n_exp, 8, rows), F32),
                pltpu.VMEM((n_exp, slot, 2 * pad), BF16),
                pltpu.VMEM((n_exp, slot, 2 * pad), BF16),
                dma((7,)),
                dma,
                dma,
                dma,
                dma((nz,)),
                dma,
                dma((nz,)),
                dma,
                dma((3,)),
                dma,
                dma,
                dma,
                dma,
                dma,
                dma((nz,)),
                dma,
                dma((nz,)),
                dma,
                dma,
                dma,
                dma,
                dma,
                dma,
                dma,
                dma,
            ],
            compiler_params=pltpu.CompilerParams(
                collective_id=0, has_side_effects=True, vmem_limit_bytes=60 * 1024 * 1024
            ),
        )(tokens, expert_ids.T, gate_logits.T, *weights, out_grad)
        mixed, in_grad, logit_grad, gate_grad, up_grad, down_grad = pl.pallas_call(
            hand_over,
            out_shape=shapes,
            in_specs=[vmem] * 6,
            out_specs=[hbm] * 6,
            scratch_shapes=[dma((6,))],
            compiler_params=pltpu.CompilerParams(vmem_limit_bytes=4 * 1024 * 1024),
        )(*outs)
        return mixed, in_grad, logit_grad.T, gate_grad[None], up_grad[None], down_grad[None]

    return jax.shard_map(
        on_device,
        mesh=mesh,
        in_specs=(
            P(("dp", "expert"), "tensor"),
            P(("dp", "expert"), None),
            P(("dp", "expert"), None),
            P("expert", None, "tensor"),
            P("expert", None, "tensor"),
            P("expert", None, "tensor"),
            P(("dp", "expert"), "tensor"),
        ),
        out_specs=(
            P(("dp", "expert"), "tensor"),
            P(("dp", "expert"), "tensor"),
            P(("dp", "expert"), None),
            P("expert", "dp", "tensor"),
            P("expert", "dp", "tensor"),
            P("expert", "dp", "tensor"),
        ),
        check_vma=False,
    )
```
